256 devices in a mesh: row: 16 (over x, y), col: 16 (over z, core).
Axes of the slice: x: 4, y: 4, z: 8, core: 2. Of those that a mesh axis runs over, the one named last changes fastest.
Arguments:
- stiff: bfloat16 [8192, 8192], P('row', 'col'), may hold values from -1 to 6, as said below
- mass: bfloat16 [8192, 8192], P('row', 'col'), may hold values from -1 to 4, as said below
- partner_row: int32 [16], replicated, may hold values from 0 to 15, as said below
- partner_col: int32 [16], replicated, may hold values from 0 to 15, as said below
- shared_one: int32 [16, 16, 2], P(None, 'col'), may hold values from 0 to 3, as said below
- shared_two: int32 [16, 16, 2], replicated, may hold values from 0 to 3, as said below
Outputs:
- grand_stiff: float32 [2048, 8192], P('row', 'col')
- grand_mass: float32 [2048, 8192], P('row', 'col')
- child_basis: float32 [8192, 8192], P('row', 'col')
The draws below stay inside these ranges and needn't reach their ends.
Inputs may be any that keep to these rules, and one draw needn't show every extreme that they name: partner_row[partner_row[i]] = i and partner_row[i] != i for every i. partner_col[partner_col[i]] = i and partner_col[i] != i for every i. `shared_one`: each list holds 2 different block numbers. `shared_two`: each list holds 2 different block numbers; only the lists at a first child's row are read. `stiff`: every 512 x 512 block is symmetric and positive definite. `mass`: every 512 x 512 block is symmetric.
All inputs are finite; a program needn't handle non-finite values.
Results may differ from the reference program's by a relative error of at most 0.0003.
Values may be sent and summed in bfloat16 or wider, within the bound.
No kernel may reach another device: no remote copies, remote signals or barrier semaphores. Data moves between devices by JAX's collectives and lax.ppermute only.
A program may use at most 64 MiB of HBM per device.

```python
import math
import jax
import jax.numpy as jnp
from jax import lax

IFACE = 512
BLOCK = 128
SHARED = 256
QUART = 128
N_ROW = 16
N_COL = 16


def kernel_block(key, width, lowest, highest, jitter_size):
    key_points, key_nugget, key_raw = jax.random.split(key, 3)
    points = jax.random.uniform(key_points, (IFACE,), jnp.float32) * IFACE
    scaled_gap = (points[:, None] - points[None, :]) / width
    kernel = jnp.exp(-scaled_gap * scaled_gap)
    nugget = jnp.exp(jax.random.uniform(key_nugget, (IFACE,), jnp.float32, math.log(lowest), math.log(highest)))
    raw_noise = jax.random.uniform(key_raw, (IFACE, IFACE), jnp.float32, -1.0, 1.0)
    jitter = (raw_noise + raw_noise.T) * (0.5 * jitter_size / IFACE)
    return kernel + jnp.eye(IFACE, dtype=jnp.float32) * nugget[None, :] + jitter


def lay_out(blocks):
    return blocks.reshape(N_ROW, N_COL, IFACE, IFACE).transpose(0, 2, 1, 3).reshape(N_ROW * IFACE, N_COL * IFACE)


def draw_stiff(key, part):
    key = jax.random.fold_in(key, 11)
    keys = jax.random.split(key, N_ROW * N_COL)
    width, lowest, highest = (IFACE / 12.0, 0.3, 1.0)
    blocks = lax.map(lambda single: kernel_block(single, width, lowest, highest, 0.5), keys)
    return lay_out(blocks).astype(jnp.bfloat16)


def draw_mass(key, part):
    key = jax.random.fold_in(key, 12)
    keys = jax.random.split(key, N_ROW * N_COL)
    width, lowest, highest = (3.0, 0.5, 1.5)
    blocks = lax.map(lambda single: kernel_block(single, width, lowest, highest, 0.3), keys)
    return lay_out(blocks).astype(jnp.bfloat16)


def matching(key, members):
    ordering = jax.random.permutation(key, members).astype(jnp.int32)
    mates = ordering[jnp.bitwise_xor(jnp.arange(members, dtype=jnp.int32), 1)]
    return jnp.zeros((members,), jnp.int32).at[ordering].set(mates)


def block_lists(key):
    block_count = IFACE // BLOCK
    scores = jax.random.randint(key, (N_ROW, N_COL, block_count), 0, 1 << 20) * block_count + jnp.arange(block_count, dtype=jnp.int32)
    return jnp.argsort(scores, axis=-1, stable=True)[..., :block_count // 2].astype(jnp.int32)


def draw_partner_row(key, part):
    key = jax.random.fold_in(key, 21)
    return matching(key, N_ROW)


def draw_partner_col(key, part):
    key = jax.random.fold_in(key, 22)
    return matching(key, N_COL)


def draw_shared_one(key, part):
    key = jax.random.fold_in(key, 31)
    return block_lists(key)


def draw_shared_two(key, part):
    key = jax.random.fold_in(key, 32)
    return block_lists(key)


def setup_inputs(seed: int = 0) -> dict:
    splits = jax.random.split(jax.random.key(seed), 7)
    stiff = draw_stiff(jax.random.fold_in(splits[6], 71), 0)
    mass = draw_mass(jax.random.fold_in(splits[6], 71), 0)
    partner_row = draw_partner_row(jax.random.fold_in(splits[6], 71), 0)
    partner_col = draw_partner_col(jax.random.fold_in(splits[6], 71), 0)
    shared_one = draw_shared_one(jax.random.fold_in(splits[6], 71), 0)
    shared_two = draw_shared_two(jax.random.fold_in(splits[6], 71), 0)
    return dict(stiff=stiff, mass=mass, partner_row=partner_row, partner_col=partner_col, shared_one=shared_one, shared_two=shared_two)


def mult(left_side, right_side):
    return jnp.dot(left_side.astype(jnp.float32), right_side.astype(jnp.float32), precision=lax.Precision.HIGHEST, preferred_element_type=jnp.float32)

def outer_blocks(shared):
    block_count = IFACE // BLOCK
    shared_marks = jnp.any(jnp.arange(block_count, dtype=jnp.int32)[:, None] == shared[None, :], axis=1).astype(jnp.int32)
    return jnp.argsort(shared_marks, stable=True)[:block_count - shared.shape[0]].astype(jnp.int32)

def pick(matrix, row_blocks, col_blocks):
    tile_view = matrix.reshape(matrix.shape[0] // BLOCK, BLOCK, matrix.shape[1] // BLOCK, BLOCK)
    chosen = tile_view[row_blocks][:, :, col_blocks]
    return chosen.reshape(row_blocks.shape[0] * BLOCK, col_blocks.shape[0] * BLOCK)

def block_diag(upper_left, lower_right):
    zero_right = jnp.zeros((upper_left.shape[0], lower_right.shape[1]), jnp.float32)
    zero_left = jnp.zeros((lower_right.shape[0], upper_left.shape[1]), jnp.float32)
    top_rows = jnp.concatenate([upper_left, zero_right], axis=1)
    bottom_rows = jnp.concatenate([zero_left, lower_right], axis=1)
    return jnp.concatenate([top_rows, bottom_rows], axis=0)

def condense(first_k, first_m, first_sh, second_k, second_m, second_sh):
    first_out = outer_blocks(first_sh)
    second_out = outer_blocks(second_sh)
    stiff_sh = pick(first_k, first_sh, first_sh) + pick(second_k, second_sh, second_sh)
    coupling = jnp.concatenate([pick(first_k, first_sh, first_out), pick(second_k, second_sh, second_out)], axis=1)
    stiff_oo = block_diag(pick(first_k, first_out, first_out), pick(second_k, second_out, second_out))
    mass_sh = pick(first_m, first_sh, first_sh) + pick(second_m, second_sh, second_sh)
    mass_cp = jnp.concatenate([pick(first_m, first_sh, first_out), pick(second_m, second_sh, second_out)], axis=1)
    mass_oo = block_diag(pick(first_m, first_out, first_out), pick(second_m, second_out, second_out))
    factor = jnp.linalg.cholesky(stiff_sh)
    reduced = jax.scipy.linalg.solve_triangular(factor, coupling, lower=True)
    recovery = jax.scipy.linalg.solve_triangular(factor, reduced, lower=True, trans=1)
    parent_k = stiff_oo - mult(reduced.T, reduced)
    cross = mult(mass_cp.T, recovery)
    parent_m = mass_oo - cross - cross.T + mult(recovery.T, mult(mass_sh, recovery))
    return (parent_k, parent_m, recovery)

def reorder_rows(stacked, block_order):
    inverse = jnp.argsort(block_order).astype(jnp.int32)
    return stacked.reshape(IFACE // BLOCK, BLOCK, stacked.shape[1])[inverse].reshape(stacked.shape)

def reference(stiff, mass, partner_row, partner_col, shared_one, shared_two):
    k_tiles = stiff.reshape(N_ROW, IFACE, N_COL, IFACE)
    m_tiles = mass.reshape(N_ROW, IFACE, N_COL, IFACE)
    rows_all = jnp.arange(N_ROW, dtype=jnp.int32)
    cols_all = jnp.arange(N_COL, dtype=jnp.int32)
    first_rows = jnp.argsort(jnp.where(rows_all < partner_row, rows_all, rows_all + N_ROW), stable=True)[:N_ROW // 2].astype(jnp.int32)
    first_cols = jnp.argsort(jnp.where(cols_all < partner_col, cols_all, cols_all + N_COL), stable=True)[:N_COL // 2].astype(jnp.int32)
    quad_rows = jnp.repeat(first_rows, N_COL // 2)
    quad_cols = jnp.tile(first_cols, N_ROW // 2)

    def quartet(indices):
        row_first, col_first = indices
        row_other = partner_row[row_first]
        col_other = partner_col[col_first]
        parents = []
        for col_at in (col_first, col_other):
            parents.append(condense(k_tiles[row_first, :, col_at, :].astype(jnp.float32), m_tiles[row_first, :, col_at, :].astype(jnp.float32), shared_one[row_first, col_at], k_tiles[row_other, :, col_at, :].astype(jnp.float32), m_tiles[row_other, :, col_at, :].astype(jnp.float32), shared_one[row_other, col_at]))
        grand_k, grand_m, recovery_two = condense(parents[0][0], parents[0][1], shared_two[row_first, col_first], parents[1][0], parents[1][1], shared_two[row_first, col_other])
        bases = []
        for side_col, col_at in enumerate((col_first, col_other)):
            list_two = shared_two[row_first, col_at]
            out_two = outer_blocks(list_two)
            placed = jnp.eye(SHARED, IFACE, k=side_col * SHARED, dtype=jnp.float32)
            stacked = jnp.concatenate([placed, -recovery_two], axis=0)
            spread = reorder_rows(stacked, jnp.concatenate([out_two, list_two]))
            shared_rows = -mult(parents[side_col][2], spread)
            for side_row, row_at in enumerate((row_first, row_other)):
                list_one = shared_one[row_at, col_at]
                out_one = outer_blocks(list_one)
                child_stack = jnp.concatenate([spread[side_row * SHARED:(side_row + 1) * SHARED], shared_rows], axis=0)
                bases.append(reorder_rows(child_stack, jnp.concatenate([out_one, list_one])))
        return (grand_k, grand_m, jnp.stack(bases))
    grand_k, grand_m, bases = lax.map(quartet, (quad_rows, quad_cols))
    quad_count = quad_rows.shape[0]
    mate_rows = partner_row[quad_rows]
    mate_cols = partner_col[quad_cols]
    row_index = jnp.stack([quad_rows, mate_rows, quad_rows, mate_rows], axis=1)
    col_index = jnp.stack([quad_cols, quad_cols, mate_cols, mate_cols], axis=1)
    placed_k = jnp.zeros((N_ROW, N_COL, QUART, IFACE), jnp.float32).at[row_index, col_index].set(grand_k.reshape(quad_count, 4, QUART, IFACE))
    placed_m = jnp.zeros((N_ROW, N_COL, QUART, IFACE), jnp.float32).at[row_index, col_index].set(grand_m.reshape(quad_count, 4, QUART, IFACE))
    placed_b = jnp.zeros((N_ROW, N_COL, IFACE, IFACE), jnp.float32).at[row_index, col_index].set(bases)
    grand_stiff = placed_k.transpose(0, 2, 1, 3).reshape(N_ROW * QUART, N_COL * IFACE)
    grand_mass = placed_m.transpose(0, 2, 1, 3).reshape(N_ROW * QUART, N_COL * IFACE)
    child_basis = placed_b.transpose(0, 2, 1, 3).reshape(N_ROW * IFACE, N_COL * IFACE)
    return (grand_stiff, grand_mass, child_basis)
```

```python
import functools

import jax
import jax.numpy as jnp
from jax import lax
from jax.experimental import pallas as pl
from jax.experimental.pallas import tpu as pltpu
from jax.sharding import PartitionSpec as P

B = 128
BF = jnp.bfloat16
F32 = jnp.float32
BOUND_RATIO = 160.0
FIXED_STEPS = 6
RESIDUAL_GOAL = 2e-3
MOST_STEPS = 40

VMEM = pl.BlockSpec(memory_space=pltpu.VMEM)
SMEM = pl.BlockSpec(memory_space=pltpu.SMEM)
PARAMS = pltpu.CompilerParams(vmem_limit_bytes=40 * 1024 * 1024)

SHARED_PAIRS = ((0, 0), (0, 1), (1, 1))
CROSS_PAIRS = ((0, 2), (0, 3), (1, 2), (1, 3))
OUTER_PAIRS = ((2, 2), (2, 3), (3, 3))


def pieces(x, count):
    out = []
    for _ in range(count - 1):
        top = x.astype(BF)
        out.append(top)
        x = x - top.astype(F32)
    out.append(x.astype(BF))
    return out


def mm(left, right, order):
    total = None
    for level in range(order, -1, -1):
        for i in range(len(left)):
            j = level - i
            if 0 <= j < len(right):
                term = jnp.dot(left[i], right[j], preferred_element_type=F32)
                total = term if total is None else total + term
    return total


def identity(n):
    return (
        lax.broadcasted_iota(jnp.int32, (n, n), 0) == lax.broadcasted_iota(jnp.int32, (n, n), 1)
    ).astype(F32)


def row_norm(x):
    return jnp.max(jnp.sum(jnp.abs(x), axis=0, keepdims=True), axis=1, keepdims=True)


def solve(a, c, c_pieces, r_ref, x_ref, j_ref):
    n = a.shape[0]
    eye = identity(n)
    picked = a * eye
    down = lax.rsqrt(jnp.sum(picked, axis=1, keepdims=True))
    across = lax.rsqrt(jnp.sum(picked, axis=0, keepdims=True))
    scaled = a * down * across
    j_ref[...] = scaled
    alpha = 2.0 / (row_norm(scaled) * (1.0 + 1.0 / BOUND_RATIO))
    r_ref[...] = eye - alpha * scaled
    x_ref[...] = alpha * eye

    def step(_, t):
        r, x = r_ref[...], x_ref[...]
        rp, xp = pieces(r, 2), pieces(x, 2)
        stacked = [jnp.concatenate([rp[k], xp[k]], axis=0) for k in range(2)]
        prod = mm(stacked, rp, 1)
        t_next = 2.0 * t * t - 1.0
        extra = 1.0 / t_next
        r_ref[...] = prod[:n] * (1.0 + extra) - extra * eye
        x_ref[...] = (x + prod[n:]) * (1.0 + extra)
        return t_next

    first = (BOUND_RATIO + 1.0) / (BOUND_RATIO - 1.0)
    lax.fori_loop(0, FIXED_STEPS, step, jnp.full((1, 1), first, F32))

    def unfinished(state):
        count, norm = state
        return (norm > RESIDUAL_GOAL) & (count < MOST_STEPS)

    def newton(state):
        count, _ = state
        x = x_ref[...]
        xp = pieces(x, 3)
        r = eye - mm(pieces(j_ref[...], 3), xp, 2)
        x_ref[...] = x + mm(xp, pieces(r, 3), 2)
        norm = jnp.max(row_norm(r))
        return count + 1, jnp.where(norm < 1.0, norm * norm, norm)

    lax.while_loop(unfinished, newton, (jnp.int32(0), jnp.max(row_norm(r_ref[...]))))

    inverse = pieces(x_ref[...] * down * across, 2)
    y = mm(inverse, c_pieces, 1)
    rest = c - mm(pieces(a, 3), pieces(y, 3), 2)
    return y + mm(inverse, pieces(rest, 2), 1)


def others(h0, h1):
    def has(k):
        return (h0 == k) | (h1 == k)

    low = jnp.where(has(0), jnp.where(has(1), 2, 1), 0)
    return low, 6 - h0 - h1 - low


def block_order(list_ref, at):
    h0, h1 = list_ref[2 * at], list_ref[2 * at + 1]
    return (h0, h1) + others(h0, h1)


def places(row_axis, col_axis, prow, pcol, one, two):
    row, col = lax.axis_index(row_axis), lax.axis_index(col_axis)
    mate, col_mate = prow[row], pcol[col]
    a = (row > mate).astype(jnp.int32)
    b = (col > col_mate).astype(jnp.int32)
    order_one = block_order(one, row)
    order_two = block_order(two, jnp.minimum(row, mate) * pcol.shape[0] + col)
    return a, b, order_one, order_two


def at_block(k):
    return pl.ds(pl.multiple_of(k * B, B), B)


def symmetric(blocks):
    d0, off, d1 = blocks
    return jnp.concatenate(
        [jnp.concatenate([d0, off], axis=1), jnp.concatenate([off.T, d1], axis=1)], axis=0
    )


def square(blocks):
    w, x, y, z = blocks
    return jnp.concatenate(
        [jnp.concatenate([w, x], axis=1), jnp.concatenate([y, z], axis=1)], axis=0
    )


def unpacked(ref, start, count):
    return [ref[(start + k) * B : (start + k + 1) * B, :].astype(F32) for k in range(count)]


def ordered(second, own, mate):
    return jnp.concatenate([jnp.where(second, mate, own), jnp.where(second, own, mate)], axis=1)


def outer_diag(second, own_ref, mate_ref):
    own, mate = symmetric(unpacked(own_ref, 7, 3)), symmetric(unpacked(mate_ref, 7, 3))
    zero = jnp.zeros((2 * B, 2 * B), F32)
    top = jnp.concatenate([jnp.where(second, mate, own), zero], axis=1)
    bottom = jnp.concatenate([zero, jnp.where(second, own, mate)], axis=1)
    return jnp.concatenate([top, bottom], axis=0)


def hand_out(full_ref, a, order_two, pay_ref, rows_ref):
    for k, (i, j) in enumerate(SHARED_PAIRS + CROSS_PAIRS):
        pay_ref[k * B : (k + 1) * B, :] = full_ref[at_block(order_two[i]), at_block(order_two[j])]
    mine = jnp.where(a == 1, order_two[3], order_two[2])
    for k in range(2):
        rows_ref[:, k * B : (k + 1) * B] = full_ref[at_block(mine), at_block(order_two[2 + k])]


def pack_kernel(axes, prow, pcol, one, two, k_ref, m_ref, out_ref):
    _, _, order, _ = places(*axes, prow, pcol, one, two)
    for k, (i, j) in enumerate(SHARED_PAIRS + CROSS_PAIRS + OUTER_PAIRS):
        out_ref[0, k * B : (k + 1) * B, :] = k_ref[at_block(order[i]), at_block(order[j])]
        out_ref[1, k * B : (k + 1) * B, :] = m_ref[at_block(order[i]), at_block(order[j])]


def stiff_one_kernel(
    axes, prow, pcol, one, two, own, mate, x1_ref, pay_ref, rows_ref, r_ref, x_ref, j_ref, full_ref
):
    own, mate = own.at[0], mate.at[0]
    a, _, _, order_two = places(*axes, prow, pcol, one, two)
    second = a == 1
    ks = symmetric([p + q for p, q in zip(unpacked(own, 0, 3), unpacked(mate, 0, 3))])
    c = ordered(second, square(unpacked(own, 3, 4)), square(unpacked(mate, 3, 4)))
    x = solve(ks, c, [c.astype(BF)], r_ref, x_ref, j_ref)
    x1_ref[...] = x
    full_ref[...] = outer_diag(second, own, mate) - mm([c.T.astype(BF)], pieces(x, 3), 2)
    hand_out(full_ref, a, order_two, pay_ref, rows_ref)


def mass_one_kernel(
    axes, prow, pcol, one, two, own, mate, x1_ref, pay_k_ref, pay_ref, rows_ref, full_ref
):
    own, mate = own.at[1], mate.at[1]
    pay_ref[0] = pay_k_ref[...]
    a, _, _, order_two = places(*axes, prow, pcol, one, two)
    second = a == 1
    ms = symmetric([p + q for p, q in zip(unpacked(own, 0, 3), unpacked(mate, 0, 3))])
    d = ordered(second, square(unpacked(own, 3, 4)), square(unpacked(mate, 3, 4)))
    x = x1_ref[...]
    xp = pieces(x, 2)
    w = mm(pieces(ms, 2), xp, 1) - d
    full_ref[...] = (
        outer_diag(second, own, mate)
        + mm(pieces(x.T, 2), pieces(w, 2), 1)
        - mm([d.T.astype(BF)], xp, 1)
    )
    hand_out(full_ref, a, order_two, pay_ref.at[1], rows_ref)


def set_in(second, part):
    zero = jnp.zeros_like(part)
    return jnp.concatenate([jnp.where(second, zero, part), jnp.where(second, part, zero)], axis=1)


def stiff_two_kernel(
    axes, prow, pcol, one, two, own, mate, rows_ref, x1_ref,
    out_ref, basis_ref, x2_ref, r_ref, x_ref, j_ref, spread_ref,
):
    own, mate = own.at[0], mate.at[0]
    a, b, order_one, order_two = places(*axes, prow, pcol, one, two)
    second = b == 1
    ks = symmetric([p + q for p, q in zip(unpacked(own, 0, 3), unpacked(mate, 0, 3))])
    c = ordered(second, square(unpacked(own, 3, 4)), square(unpacked(mate, 3, 4)))
    x = solve(ks, c, pieces(c, 2), r_ref, x_ref, j_ref)
    x2_ref[...] = x
    xp = pieces(x, 2)
    c_mine = jnp.concatenate([own[at_block(3 + a), :], own[at_block(5 + a), :]], axis=0)
    out_ref[...] = set_in(second, rows_ref[...]) - mm(pieces(c_mine.T, 2), xp, 1)

    eye = identity(B)
    zero = jnp.zeros((B, B), F32)
    for k in range(2):
        spread_ref[at_block(order_two[k]), :] = -x[k * B : (k + 1) * B, :]
        half = jnp.concatenate([eye if k == 0 else zero, eye if k == 1 else zero], axis=1)
        spread_ref[at_block(order_two[2 + k]), :] = set_in(second, half)
    for k in range(2):
        basis_ref[at_block(order_one[2 + k]), :] = spread_ref[at_block(2 * a + k), :]
    x1_sh = jnp.concatenate([x1_ref[:, at_block(order_two[k])] for k in range(2)], axis=1)
    x1_out = jnp.concatenate([x1_ref[:, at_block(order_two[2 + k])] for k in range(2)], axis=1)
    shared = mm(pieces(x1_sh, 2), xp, 1) - set_in(second, x1_out)
    for k in range(2):
        basis_ref[at_block(order_one[k]), :] = shared[k * B : (k + 1) * B, :]


def mass_two_kernel(axes, prow, pcol, one, two, own, mate, rows_ref, x2_ref, out_ref):
    own, mate = own.at[1], mate.at[1]
    a, b, _, _ = places(*axes, prow, pcol, one, two)
    second = b == 1
    ms = symmetric([p + q for p, q in zip(unpacked(own, 0, 3), unpacked(mate, 0, 3))])
    d = ordered(second, square(unpacked(own, 3, 4)), square(unpacked(mate, 3, 4)))
    xp = pieces(x2_ref[...], 2)
    w = mm(pieces(ms, 2), xp, 1) - d
    x_mine = x2_ref[:, at_block(2 * b + a)]
    d_mine = jnp.concatenate([own[at_block(3 + a), :], own[at_block(5 + a), :]], axis=0)
    out_ref[...] = (
        set_in(second, rows_ref[...])
        + mm(pieces(x_mine.T, 2), pieces(w, 2), 1)
        - mm(pieces(d_mine.T, 2), xp, 1)
    )


def call(kernel, axes, outs, scratch, meta, arrays, cost):
    return pl.pallas_call(
        functools.partial(kernel, axes),
        out_shape=[jax.ShapeDtypeStruct(shape, dtype) for shape, dtype in outs],
        in_specs=[SMEM] * len(meta) + [VMEM] * len(arrays),
        out_specs=[VMEM] * len(outs),
        scratch_shapes=[pltpu.VMEM(shape, F32) for shape in scratch],
        compiler_params=PARAMS,
        cost_estimate=pl.CostEstimate(flops=cost, bytes_accessed=1 << 20, transcendentals=0),
    )(*meta, *arrays)


def swap(axis, partner, array):
    size = partner.shape[0]
    me = lax.axis_index(axis)

    def branch(gap):
        return lambda y: lax.ppermute(y, axis, [(i, i ^ gap) for i in range(size)])

    return lax.switch((me ^ partner[me]) - 1, [branch(gap) for gap in range(1, size)], array)


def local(stiff, mass, partner_row, partner_col, shared_one, shared_two):
    axes = ("row", "col")
    meta = (partner_row, partner_col, shared_one.reshape(-1), shared_two.reshape(-1))
    iface = stiff.shape[0]
    half = iface // 2
    square_half = (half, half)
    raw, pay = (10 * B, B), (7 * B, B)

    (packed,) = call(pack_kernel, axes, [((2, *raw), BF)], [], meta, (stiff, mass), 1 << 20)
    mate = swap("row", partner_row, packed)
    x1, pay_k, rows_k = call(
        stiff_one_kernel, axes,
        [((half, iface), F32), (pay, F32), ((B, half), F32)],
        [square_half] * 3 + [(iface, iface)],
        meta, (packed, mate), 6 << 30,
    )
    both, rows_m = call(
        mass_one_kernel, axes, [((2, *pay), F32), ((B, half), F32)], [(iface, iface)],
        meta, (packed, mate, x1, pay_k), 1 << 30,
    )
    mate_both = swap("col", partner_col, both)
    grand_stiff, child_basis, x2 = call(
        stiff_two_kernel, axes,
        [((B, iface), F32), ((iface, iface), F32), ((half, iface), F32)],
        [square_half] * 3 + [(iface, iface)],
        meta, (both, mate_both, rows_k, x1), 6 << 30,
    )
    (grand_mass,) = call(
        mass_two_kernel, axes, [((B, iface), F32)], [],
        meta, (both, mate_both, rows_m, x2), 1 << 30,
    )
    return grand_stiff, grand_mass, child_basis


def solution(mesh):
    return jax.shard_map(
        local,
        mesh=mesh,
        in_specs=(P("row", "col"), P("row", "col"), P(), P(), P(None, "col", None), P()),
        out_specs=(P("row", "col"), P("row", "col"), P("row", "col")),
        check_vma=False,
    )
```

```python
import functools

import jax
import jax.numpy as jnp
from jax import lax
from jax.experimental import pallas as pl
from jax.experimental.pallas import tpu as pltpu
from jax.sharding import PartitionSpec as P

B = 128
BF = jnp.bfloat16
F32 = jnp.float32
BOUND_RATIO = 160.0
FIXED_STEPS = 6
RESIDUAL_GOAL = 2e-3
MOST_STEPS = 40

VMEM = pl.BlockSpec(memory_space=pltpu.VMEM)
SMEM = pl.BlockSpec(memory_space=pltpu.SMEM)
PARAMS = pltpu.CompilerParams(vmem_limit_bytes=40 * 1024 * 1024)

SHARED, OUTER = (0, 1), (2, 3)
CROSS = ((0, 2), (0, 3), (1, 2), (1, 3))
TAIL = 16
RAW_ROWS = 8 * B + TAIL
CODED = 6
CODE_ROWS = CODED * B + CODED // 2 * B + TAIL
LOW = 256
TOP_BITS = 23


def pieces(x, count):
    out = []
    for _ in range(count - 1):
        top = x.astype(BF)
        out.append(top)
        x = x - top.astype(F32)
    out.append(x.astype(BF))
    return out


def mm(left, right, order):
    total = None
    for level in range(order, -1, -1):
        for i in range(len(left)):
            j = level - i
            if 0 <= j < len(right):
                term = jnp.dot(left[i], right[j], preferred_element_type=F32)
                total = term if total is None else total + term
    return total


def identity(n):
    return (
        lax.broadcasted_iota(jnp.int32, (n, n), 0) == lax.broadcasted_iota(jnp.int32, (n, n), 1)
    ).astype(F32)


def row_norm(x):
    return jnp.max(jnp.sum(jnp.abs(x), axis=0, keepdims=True), axis=1, keepdims=True)


def solve(a, c, c_pieces, r_ref, x_ref, j_ref):
    n = a.shape[0]
    eye = identity(n)
    picked = a * eye
    down = lax.rsqrt(jnp.sum(picked, axis=1, keepdims=True))
    across = lax.rsqrt(jnp.sum(picked, axis=0, keepdims=True))
    scaled = a * down * across
    j_ref[...] = scaled
    alpha = 2.0 / (row_norm(scaled) * (1.0 + 1.0 / BOUND_RATIO))
    r_ref[...] = eye - alpha * scaled
    x_ref[...] = alpha * eye

    def step(_, t):
        r, x = r_ref[...], x_ref[...]
        rp, xp = pieces(r, 2), pieces(x, 2)
        stacked = [jnp.concatenate([rp[k], xp[k]], axis=0) for k in range(2)]
        prod = mm(stacked, rp, 1)
        t_next = 2.0 * t * t - 1.0
        extra = 1.0 / t_next
        r_ref[...] = prod[:n] * (1.0 + extra) - extra * eye
        x_ref[...] = (x + prod[n:]) * (1.0 + extra)
        return t_next

    first = (BOUND_RATIO + 1.0) / (BOUND_RATIO - 1.0)
    lax.fori_loop(0, FIXED_STEPS, step, jnp.full((1, 1), first, F32))

    def unfinished(state):
        count, norm = state
        return (norm > RESIDUAL_GOAL) & (count < MOST_STEPS)

    def newton(state):
        count, _ = state
        x = x_ref[...]
        xp = pieces(x, 3)
        r = eye - mm(pieces(j_ref[...], 3), xp, 2)
        x_ref[...] = x + mm(xp, pieces(r, 3), 2)
        norm = jnp.max(row_norm(r))
        return count + 1, jnp.where(norm < 1.0, norm * norm, norm)

    lax.while_loop(unfinished, newton, (jnp.int32(0), jnp.max(row_norm(r_ref[...]))))

    inverse = pieces(x_ref[...] * down * across, 2)
    y = mm(inverse, c_pieces, 1)
    rest = c - mm(pieces(a, 3), pieces(y, 3), 2)
    return y + mm(inverse, pieces(rest, 2), 1)


def others(h0, h1):
    def has(k):
        return (h0 == k) | (h1 == k)

    low = jnp.where(has(0), jnp.where(has(1), 2, 1), 0)
    return low, 6 - h0 - h1 - low


def block_order(list_ref, at):
    h0, h1 = list_ref[2 * at], list_ref[2 * at + 1]
    return (h0, h1) + others(h0, h1)


def places(row_axis, col_axis, prow, pcol, one, two):
    row, col = lax.axis_index(row_axis), lax.axis_index(col_axis)
    mate, col_mate = prow[row], pcol[col]
    a = (row > mate).astype(jnp.int32)
    b = (col > col_mate).astype(jnp.int32)
    order_one = block_order(one, row)
    order_two = block_order(two, jnp.minimum(row, mate) * pcol.shape[0] + col)
    return a, b, order_one, order_two


def at_block(k):
    return pl.ds(pl.multiple_of(k * B, B), B)


def triangles():
    rows = lax.broadcasted_iota(jnp.int32, (B, B), 0)
    cols = lax.broadcasted_iota(jnp.int32, (B, B), 1)
    return rows, cols


def paired(first, second):
    rows, cols = triangles()
    return jnp.where(rows >= cols, first, second)


def diagonal(block):
    rows, cols = triangles()
    return jnp.sum(jnp.where(rows == cols, block, 0.0), axis=0, keepdims=True)


def unpaired(pair, diag):
    rows, cols = triangles()
    turned = pair.T
    first = jnp.where(rows >= cols, pair, turned)
    second = jnp.where(rows == cols, diag, jnp.where(rows < cols, pair, turned))
    return first, second


def symmetric(pair, off, diag):
    d0, d1 = unpaired(pair, diag)
    return square((d0, off, off.T, d1))


def square(blocks):
    w, x, y, z = blocks
    return jnp.concatenate(
        [jnp.concatenate([w, x], axis=1), jnp.concatenate([y, z], axis=1)], axis=0
    )


def block(ref, k):
    return ref[k * B : (k + 1) * B, :].astype(F32)


def tail(ref, start, k):
    return ref[start : start + TAIL, :].astype(F32)[k : k + 1, :]


def raw_shared(ref):
    return symmetric(block(ref, 0), block(ref, 1), tail(ref, 8 * B, 0))


def raw_cross(ref):
    return square([block(ref, 2 + k) for k in range(4)])


def raw_outer(ref):
    return symmetric(block(ref, 6), block(ref, 7), tail(ref, 8 * B, 1))


def ordered(second, own, mate):
    return jnp.concatenate([jnp.where(second, mate, own), jnp.where(second, own, mate)], axis=1)


def outer_diag(second, own_ref, mate_ref):
    own, mate = raw_outer(own_ref), raw_outer(mate_ref)
    zero = jnp.zeros((2 * B, 2 * B), F32)
    top = jnp.concatenate([jnp.where(second, mate, own), zero], axis=1)
    bottom = jnp.concatenate([zero, jnp.where(second, own, mate)], axis=1)
    return jnp.concatenate([top, bottom], axis=0)


def tail_rows(rows):
    at = lax.broadcasted_iota(jnp.int32, (TAIL, B), 0)
    out = jnp.zeros((TAIL, B), rows[0].dtype)
    for k, row in enumerate(rows):
        out = jnp.where(at == k, row, out)
    return out


def encode(blocks, diag, code_ref):
    largest = jnp.max(jnp.abs(diag), axis=1, keepdims=True)
    for x in blocks:
        top = jnp.max(jnp.max(jnp.abs(x), axis=0, keepdims=True), axis=1, keepdims=True)
        largest = jnp.maximum(largest, top)
    power = jnp.ceil(jnp.log2(jnp.clip(largest, 1e-30, 1e30)) + 2e-3)
    scale = jnp.exp2(TOP_BITS - power)

    def parts(x):
        whole = jnp.floor(x * scale + 0.5).astype(jnp.int32)
        high = whole >> 8
        return high, whole - high * LOW

    for k in range(0, CODED, 2):
        (high_a, low_a), (high_b, low_b) = parts(blocks[k]), parts(blocks[k + 1])
        code_ref[k * B : (k + 1) * B, :] = high_a.astype(jnp.int16)
        code_ref[(k + 1) * B : (k + 2) * B, :] = high_b.astype(jnp.int16)
        at = CODED * B + k // 2 * B
        code_ref[at : at + B, :] = (low_a * LOW + low_b - LOW * LOW // 2).astype(jnp.int16)
    high, low = parts(diag)
    exponent = jnp.zeros((1, B), jnp.int32) + power.astype(jnp.int32)
    code_ref[CODE_ROWS - TAIL : CODE_ROWS, :] = tail_rows([high, low, exponent]).astype(jnp.int16)


def decode(code_ref):
    end = code_ref[CODE_ROWS - TAIL : CODE_ROWS, :].astype(jnp.int32)
    unit = jnp.exp2(end[2:3, 0:1].astype(F32) - TOP_BITS)

    def value(high, low):
        return (high * LOW + low).astype(F32) * unit

    blocks = []
    for k in range(0, CODED, 2):
        at = CODED * B + k // 2 * B
        lows = code_ref[at : at + B, :].astype(jnp.int32) + LOW * LOW // 2
        low_a = lows >> 8
        for m, low in enumerate((low_a, lows - low_a * LOW)):
            high = code_ref[(k + m) * B : (k + m + 1) * B, :].astype(jnp.int32)
            blocks.append(value(high, low))
    return symmetric(blocks[0], blocks[1], value(end[0:1, :], end[1:2, :])), square(blocks[2:])


def hand_out(full_ref, a, order, code_ref, shared_ref, cross_ref, rows_ref):
    d0, off, d1 = [
        full_ref[at_block(order[i]), at_block(order[j])] for i, j in ((0, 0), (0, 1), (1, 1))
    ]
    cross = [full_ref[at_block(order[i]), at_block(order[j])] for i, j in CROSS]
    shared_ref[...] = square((d0, off, off.T, d1))
    cross_ref[...] = square(cross)
    encode([paired(d0, d1), off] + cross, diagonal(d1), code_ref)
    mine = jnp.where(a == 1, order[3], order[2])
    for k in range(2):
        rows_ref[:, k * B : (k + 1) * B] = full_ref[at_block(mine), at_block(order[2 + k])]


def pack_kernel(axes, prow, pcol, one, two, k_hbm, m_hbm, out_ref, gap_ref, held_ref, sems):
    row, col = lax.axis_index(axes[0]), lax.axis_index(axes[1])
    gap_ref[0] = (row ^ prow[row]) - 1
    gap_ref[1] = (col ^ pcol[col]) - 1
    order = block_order(one, row)
    copies = []
    for which, source in enumerate((k_hbm, m_hbm)):
        targets = [(held_ref.at[which, k], k, k) for k in range(4)]
        for at, (i, j) in ((1, SHARED), (7, OUTER), *((2 + k, pair) for k, pair in enumerate(CROSS))):
            targets.append((out_ref.at[which, at * B : (at + 1) * B, :], i, j))
        for target, i, j in targets:
            copies.append(
                pltpu.make_async_copy(
                    source.at[at_block(order[i]), at_block(order[j])], target, sems.at[len(copies)]
                )
            )
            copies[-1].start()
    for copy in copies:
        copy.wait()
    for which in range(2):
        s0, s1, o0, o1 = [held_ref[which, k].astype(F32) for k in range(4)]
        out_ref[which, :B, :] = paired(s0, s1).astype(BF)
        out_ref[which, 6 * B : 7 * B, :] = paired(o0, o1).astype(BF)
        out_ref[which, 8 * B :, :] = tail_rows([diagonal(s1), diagonal(o1)]).astype(BF)


def stiff_one_kernel(
    axes, prow, pcol, one, two, own, mate,
    x1_ref, code_ref, shared_ref, cross_ref, rows_ref, r_ref, x_ref, j_ref, full_ref,
):
    own, mate = own.at[0], mate.at[0]
    a, _, _, order_two = places(*axes, prow, pcol, one, two)
    second = a == 1
    ks = raw_shared(own) + raw_shared(mate)
    c = ordered(second, raw_cross(own), raw_cross(mate))
    x = solve(ks, c, [c.astype(BF)], r_ref, x_ref, j_ref)
    x1_ref[...] = x
    full_ref[...] = outer_diag(second, own, mate) - mm([c.T.astype(BF)], pieces(x, 3), 2)
    hand_out(full_ref, a, order_two, code_ref, shared_ref, cross_ref, rows_ref)


def mass_one_kernel(
    axes, prow, pcol, one, two, own, mate, x1_ref, code_k_ref,
    code_ref, shared_ref, cross_ref, rows_ref, full_ref,
):
    own, mate = own.at[1], mate.at[1]
    code_ref[0] = code_k_ref[...]
    a, _, _, order_two = places(*axes, prow, pcol, one, two)
    second = a == 1
    ms = raw_shared(own) + raw_shared(mate)
    d = ordered(second, raw_cross(own), raw_cross(mate))
    x = x1_ref[...]
    xp = pieces(x, 2)
    w = mm(pieces(ms, 2), xp, 1) - d
    full_ref[...] = (
        outer_diag(second, own, mate)
        + mm(pieces(x.T, 2), pieces(w, 2), 1)
        - mm([d.T.astype(BF)], xp, 1)
    )
    hand_out(full_ref, a, order_two, code_ref.at[1], shared_ref, cross_ref, rows_ref)


def set_in(second, part):
    zero = jnp.zeros_like(part)
    return jnp.concatenate([jnp.where(second, zero, part), jnp.where(second, part, zero)], axis=1)


def stiff_two_kernel(
    axes, prow, pcol, one, two, shared_ref, cross_ref, mate, rows_ref, x1_ref,
    out_ref, basis_ref, x2_ref, r_ref, x_ref, j_ref, spread_ref,
):
    a, b, order_one, order_two = places(*axes, prow, pcol, one, two)
    second = b == 1
    mate_shared, mate_cross = decode(mate.at[0])
    ks = shared_ref[...] + mate_shared
    c = ordered(second, cross_ref[...], mate_cross)
    x = solve(ks, c, pieces(c, 2), r_ref, x_ref, j_ref)
    x2_ref[...] = x
    xp = pieces(x, 2)
    c_mine = cross_ref[:, at_block(a)]
    out_ref[...] = set_in(second, rows_ref[...]) - mm(pieces(c_mine.T, 2), xp, 1)

    eye = identity(B)
    zero = jnp.zeros((B, B), F32)
    for k in range(2):
        spread_ref[at_block(order_two[k]), :] = -x[k * B : (k + 1) * B, :]
        half = jnp.concatenate([eye if k == 0 else zero, eye if k == 1 else zero], axis=1)
        spread_ref[at_block(order_two[2 + k]), :] = set_in(second, half)
    for k in range(2):
        basis_ref[at_block(order_one[2 + k]), :] = spread_ref[at_block(2 * a + k), :]
    x1_sh = jnp.concatenate([x1_ref[:, at_block(order_two[k])] for k in range(2)], axis=1)
    x1_out = jnp.concatenate([x1_ref[:, at_block(order_two[2 + k])] for k in range(2)], axis=1)
    shared = mm(pieces(x1_sh, 2), xp, 1) - set_in(second, x1_out)
    for k in range(2):
        basis_ref[at_block(order_one[k]), :] = shared[k * B : (k + 1) * B, :]


def mass_two_kernel(
    axes, prow, pcol, one, two, shared_ref, cross_ref, mate, rows_ref, x2_ref, out_ref
):
    a, b, _, _ = places(*axes, prow, pcol, one, two)
    second = b == 1
    mate_shared, mate_cross = decode(mate.at[1])
    ms = shared_ref[...] + mate_shared
    d = ordered(second, cross_ref[...], mate_cross)
    xp = pieces(x2_ref[...], 2)
    w = mm(pieces(ms, 2), xp, 1) - d
    x_mine = x2_ref[:, at_block(2 * b + a)]
    d_mine = cross_ref[:, at_block(a)]
    out_ref[...] = (
        set_in(second, rows_ref[...])
        + mm(pieces(x_mine.T, 2), pieces(w, 2), 1)
        - mm(pieces(d_mine.T, 2), xp, 1)
    )


def call(kernel, axes, outs, scratch, meta, arrays, cost):
    return pl.pallas_call(
        functools.partial(kernel, axes),
        out_shape=[jax.ShapeDtypeStruct(shape, dtype) for shape, dtype in outs],
        in_specs=[SMEM] * len(meta) + [VMEM] * len(arrays),
        out_specs=[VMEM] * len(outs),
        scratch_shapes=[pltpu.VMEM(shape, F32) for shape in scratch],
        compiler_params=PARAMS,
        cost_estimate=pl.CostEstimate(flops=cost, bytes_accessed=1 << 20, transcendentals=0),
    )(*meta, *arrays)


def swap(axis, size, gap, array):
    def branch(apart):
        return lambda y: lax.ppermute(y, axis, [(i, i ^ apart) for i in range(size)])

    return lax.switch(gap, [branch(apart) for apart in range(1, size)], array)


def local(stiff, mass, partner_row, partner_col, shared_one, shared_two):
    axes = ("row", "col")
    meta = (partner_row, partner_col, shared_one.reshape(-1), shared_two.reshape(-1))
    iface = stiff.shape[0]
    half = iface // 2
    square_half = (half, half)
    code = (CODE_ROWS, B)
    kept = [(square_half, F32), (square_half, F32), ((B, half), F32)]

    packed, gaps = pl.pallas_call(
        functools.partial(pack_kernel, axes),
        out_shape=[
            jax.ShapeDtypeStruct((2, RAW_ROWS, B), BF),
            jax.ShapeDtypeStruct((2,), jnp.int32),
        ],
        in_specs=[SMEM] * 4 + [pl.BlockSpec(memory_space=pl.ANY)] * 2,
        out_specs=[VMEM, SMEM],
        scratch_shapes=[pltpu.VMEM((2, 4, B, B), BF), pltpu.SemaphoreType.DMA((20,))],
        compiler_params=PARAMS,
    )(*meta, stiff, mass)
    mate = swap("row", partner_row.shape[0], gaps[0], packed)
    x1, code_k, shared_k, cross_k, rows_k = call(
        stiff_one_kernel, axes, [((half, iface), F32), (code, jnp.int16), *kept],
        [square_half] * 3 + [(iface, iface)],
        meta, (packed, mate), 6 << 30,
    )
    codes, shared_m, cross_m, rows_m = call(
        mass_one_kernel, axes, [((2, *code), jnp.int16), *kept], [(iface, iface)],
        meta, (packed, mate, x1, code_k), 1 << 30,
    )
    mate_codes = swap("col", partner_col.shape[0], gaps[1], codes)
    grand_stiff, child_basis, x2 = call(
        stiff_two_kernel, axes,
        [((B, iface), F32), ((iface, iface), F32), ((half, iface), F32)],
        [square_half] * 3 + [(iface, iface)],
        meta, (shared_k, cross_k, mate_codes, rows_k, x1), 6 << 30,
    )
    (grand_mass,) = call(
        mass_two_kernel, axes, [((B, iface), F32)], [],
        meta, (shared_m, cross_m, mate_codes, rows_m, x2), 1 << 30,
    )
    return grand_stiff, grand_mass, child_basis


def solution(mesh):
    return jax.shard_map(
        local,
        mesh=mesh,
        in_specs=(P("row", "col"), P("row", "col"), P(), P(), P(None, "col", None), P()),
        out_specs=(P("row", "col"), P("row", "col"), P("row", "col")),
        check_vma=False,
    )
```

```python
import functools

import jax
import jax.numpy as jnp
from jax import lax
from jax.experimental import pallas as pl
from jax.experimental.pallas import tpu as pltpu
from jax.sharding import PartitionSpec as P

B = 128
BF = jnp.bfloat16
F32 = jnp.float32
BOUND_RATIO = 160.0
FIXED_STEPS = 6
RESIDUAL_GOAL = 2e-3
MOST_STEPS = 40

VMEM = pl.BlockSpec(memory_space=pltpu.VMEM)
SMEM = pl.BlockSpec(memory_space=pltpu.SMEM)
PARAMS = pltpu.CompilerParams(vmem_limit_bytes=40 * 1024 * 1024)

SHARED, OUTER = (0, 1), (2, 3)
CROSS = ((0, 2), (0, 3), (1, 2), (1, 3))
TAIL = 16
RAW_ROWS = 8 * B + TAIL
CODED = 6
HIGH_ROWS = CODED * B
K_LOW_ROWS = CODED * B // 2
M_LOW_ROWS = CODED * B // 4
K_CODE_ROWS = HIGH_ROWS + K_LOW_ROWS + TAIL
M_CODE_ROWS = HIGH_ROWS + M_LOW_ROWS + TAIL
K_BITS, M_BITS = 23, 19
SECOND_ROW, SECOND_COL, ORDER_ONE, ORDER_TWO, FACTS = 0, 1, 2, 6, 10


def pieces(x, count):
    out = []
    for _ in range(count - 1):
        top = x.astype(BF)
        out.append(top)
        x = x - top.astype(F32)
    out.append(x.astype(BF))
    return out


def mm(left, right, order):
    total = None
    for level in range(order, -1, -1):
        for i in range(len(left)):
            j = level - i
            if 0 <= j < len(right):
                term = jnp.dot(left[i], right[j], preferred_element_type=F32)
                total = term if total is None else total + term
    return total


def identity(n):
    return (
        lax.broadcasted_iota(jnp.int32, (n, n), 0) == lax.broadcasted_iota(jnp.int32, (n, n), 1)
    ).astype(F32)


def row_norm(x):
    return jnp.max(jnp.sum(jnp.abs(x), axis=0, keepdims=True), axis=1, keepdims=True)


def solve(a, c, c_pieces, r_ref, x_ref, j_ref):
    n = a.shape[0]
    eye = identity(n)
    picked = a * eye
    down = lax.rsqrt(jnp.sum(picked, axis=1, keepdims=True))
    across = lax.rsqrt(jnp.sum(picked, axis=0, keepdims=True))
    scaled = a * down * across
    j_ref[...] = scaled
    alpha = 2.0 / (row_norm(scaled) * (1.0 + 1.0 / BOUND_RATIO))
    r_ref[...] = eye - alpha * scaled
    x_ref[...] = alpha * eye

    def step(_, t):
        r, x = r_ref[...], x_ref[...]
        rp, xp = pieces(r, 2), pieces(x, 2)
        stacked = [jnp.concatenate([rp[k], xp[k]], axis=0) for k in range(2)]
        prod = mm(stacked, rp, 1)
        t_next = 2.0 * t * t - 1.0
        extra = 1.0 / t_next
        r_ref[...] = prod[:n] * (1.0 + extra) - extra * eye
        x_ref[...] = (x + prod[n:]) * (1.0 + extra)
        return t_next

    first = (BOUND_RATIO + 1.0) / (BOUND_RATIO - 1.0)
    lax.fori_loop(0, FIXED_STEPS, step, jnp.full((1, 1), first, F32))

    def unfinished(state):
        count, norm = state
        return (norm > RESIDUAL_GOAL) & (count < MOST_STEPS)

    def newton(state):
        count, _ = state
        x = x_ref[...]
        xp = pieces(x, 3)
        r = eye - mm(pieces(j_ref[...], 3), xp, 2)
        x_ref[...] = x + mm(xp, pieces(r, 3), 2)
        norm = jnp.max(row_norm(r))
        return count + 1, jnp.where(norm < 1.0, norm * norm, norm)

    lax.while_loop(unfinished, newton, (jnp.int32(0), jnp.max(row_norm(r_ref[...]))))

    inverse = pieces(x_ref[...] * down * across, 2)
    y = mm(inverse, c_pieces, 1)
    rest = c - mm(pieces(a, 3), pieces(y, 3), 2)
    return y + mm(inverse, pieces(rest, 2), 1)


def others(h0, h1):
    def has(k):
        return (h0 == k) | (h1 == k)

    low = jnp.where(has(0), jnp.where(has(1), 2, 1), 0)
    return low, 6 - h0 - h1 - low


def facts(ref):
    order_one = [ref[ORDER_ONE + k] for k in range(4)]
    order_two = [ref[ORDER_TWO + k] for k in range(4)]
    return ref[SECOND_ROW], ref[SECOND_COL], order_one, order_two


def at_block(k):
    return pl.ds(pl.multiple_of(k * B, B), B)


def triangles():
    rows = lax.broadcasted_iota(jnp.int32, (B, B), 0)
    cols = lax.broadcasted_iota(jnp.int32, (B, B), 1)
    return rows, cols


def paired(first, second):
    rows, cols = triangles()
    return jnp.where(rows >= cols, first, second)


def diagonal(block):
    rows, cols = triangles()
    return jnp.sum(jnp.where(rows == cols, block, 0.0), axis=0, keepdims=True)


def unpaired(pair, diag):
    rows, cols = triangles()
    turned = pair.T
    first = jnp.where(rows >= cols, pair, turned)
    second = jnp.where(rows == cols, diag, jnp.where(rows < cols, pair, turned))
    return first, second


def symmetric(pair, off, diag):
    d0, d1 = unpaired(pair, diag)
    return square((d0, off, off.T, d1))


def square(blocks):
    w, x, y, z = blocks
    return jnp.concatenate(
        [jnp.concatenate([w, x], axis=1), jnp.concatenate([y, z], axis=1)], axis=0
    )


def block(ref, k):
    return ref[k * B : (k + 1) * B, :].astype(F32)


def tail(ref, start, k):
    return ref[start : start + TAIL, :].astype(F32)[k : k + 1, :]


def raw_shared(ref):
    return symmetric(block(ref, 0), block(ref, 1), tail(ref, 8 * B, 0))


def raw_cross(ref):
    return square([block(ref, 2 + k) for k in range(4)])


def raw_outer(ref):
    return symmetric(block(ref, 6), block(ref, 7), tail(ref, 8 * B, 1))


def ordered(second, own, mate):
    return jnp.concatenate([jnp.where(second, mate, own), jnp.where(second, own, mate)], axis=1)


def outer_diag(second, own_ref, mate_ref):
    own, mate = raw_outer(own_ref), raw_outer(mate_ref)
    zero = jnp.zeros((2 * B, 2 * B), F32)
    top = jnp.concatenate([jnp.where(second, mate, own), zero], axis=1)
    bottom = jnp.concatenate([zero, jnp.where(second, own, mate)], axis=1)
    return jnp.concatenate([top, bottom], axis=0)


def tail_rows(rows):
    at = lax.broadcasted_iota(jnp.int32, (TAIL, B), 0)
    out = jnp.zeros((TAIL, B), rows[0].dtype)
    for k, row in enumerate(rows):
        out = jnp.where(at == k, row, out)
    return out


def whole(x, scale, bits):
    limit = 2.0**bits - 1.0
    return jnp.clip(jnp.floor(x * scale + 0.5), -limit, limit).astype(jnp.int32)


def upright(row):
    rows, cols = triangles()
    return jnp.sum(jnp.where(rows == cols, row, 0.0), axis=1, keepdims=True)


def stiff_units(exponents, sign):
    across = [jnp.exp2(sign * e) for e in exponents]
    down = [upright(across[k]) for k in range(2)]
    units = [paired(down[0] * across[0], down[1] * across[1]), down[0] * across[1]]
    units += [down[i] * across[j] for i, j in CROSS]
    return units, across[1] * across[1]


def encode_stiff(blocks, diags, ref):
    exponents = [
        jnp.ceil(0.5 * jnp.log2(jnp.clip(d, 1e-30, 1e30)) + 2e-3) for d in diags
    ]
    units, unit = stiff_units(exponents, -1.0)
    size = 2.0**K_BITS
    for k in range(0, CODED, 2):
        lows = []
        for m in (k, k + 1):
            number = whole(blocks[m], units[m] * size, K_BITS)
            ref[m * B : (m + 1) * B, :] = (number >> 8).astype(jnp.int16)
            lows.append(number & 255)
        at = HIGH_ROWS + k // 2 * B
        ref[at : at + B, :] = (lows[0] * 256 + lows[1] - 32768).astype(jnp.int16)
    number = whole(diags[1], unit * size, K_BITS)
    rows = [number >> 8, number & 255] + [e.astype(jnp.int32) for e in exponents]
    ref[K_CODE_ROWS - TAIL : K_CODE_ROWS, :] = tail_rows(rows).astype(jnp.int16)


def decode_stiff(ref):
    end = ref[K_CODE_ROWS - TAIL : K_CODE_ROWS, :].astype(jnp.int32)
    units, unit = stiff_units([end[2 + k : 3 + k, :].astype(F32) for k in range(4)], 1.0)
    size = 2.0**-K_BITS
    blocks = []
    for k in range(0, CODED, 2):
        at = HIGH_ROWS + k // 2 * B
        lows = ref[at : at + B, :].astype(jnp.int32) + 32768
        for m, low in ((k, lows >> 8), (k + 1, lows & 255)):
            high = ref[m * B : (m + 1) * B, :].astype(jnp.int32)
            blocks.append((high * 256 + low).astype(F32) * (units[m] * size))
    diag = (end[0:1, :] * 256 + end[1:2, :]).astype(F32) * (unit * size)
    return symmetric(blocks[0], blocks[1], diag), square(blocks[2:])


LOW_QUADS = (((0, 0, B), (1, 0, B), (2, 0, B), (3, 0, B)), ((4, 0, B // 2), (4, B // 2, B), (5, 0, B // 2), (5, B // 2, B)))


def encode_mass(blocks, diag, ref):
    largest = jnp.max(jnp.abs(diag), axis=1, keepdims=True)
    for x in blocks:
        top = jnp.max(jnp.max(jnp.abs(x), axis=0, keepdims=True), axis=1, keepdims=True)
        largest = jnp.maximum(largest, top)
    power = jnp.ceil(jnp.log2(jnp.clip(largest, 1e-30, 1e30)) + 2e-3)
    scale = jnp.exp2(M_BITS - power)
    lows = []
    for k in range(CODED):
        number = whole(blocks[k], scale, M_BITS)
        ref[k * B : (k + 1) * B, :] = (number >> 4).astype(jnp.int16)
        lows.append(number & 15)
    at = HIGH_ROWS
    for quad in LOW_QUADS:
        w, x, y, z = [lows[k][start:stop] for k, start, stop in quad]
        packed = ((w * 16 + x) * 16 + y) * 16 + z - 32768
        ref[at : at + packed.shape[0], :] = packed.astype(jnp.int16)
        at += packed.shape[0]
    number = whole(diag, scale, M_BITS)
    exponent = jnp.zeros((1, B), jnp.int32) + power.astype(jnp.int32)
    rows = [number >> 4, number & 15, exponent]
    ref[M_CODE_ROWS - TAIL : M_CODE_ROWS, :] = tail_rows(rows).astype(jnp.int16)


def decode_mass(ref):
    end = ref[M_CODE_ROWS - TAIL : M_CODE_ROWS, :].astype(jnp.int32)
    unit = jnp.exp2(end[2:3, 0:1].astype(F32) - M_BITS)
    first = ref[HIGH_ROWS : HIGH_ROWS + B, :].astype(jnp.int32) + 32768
    rest = ref[HIGH_ROWS + B : HIGH_ROWS + M_LOW_ROWS, :].astype(jnp.int32) + 32768
    lows = [(first >> shift) & 15 for shift in (12, 8, 4, 0)]
    halves = [(rest >> shift) & 15 for shift in (12, 8, 4, 0)]
    lows += [jnp.concatenate(halves[k : k + 2], axis=0) for k in (0, 2)]
    blocks = []
    for k in range(CODED):
        high = ref[k * B : (k + 1) * B, :].astype(jnp.int32)
        blocks.append((high * 16 + lows[k]).astype(F32) * unit)
    diag = (end[0:1, :] * 16 + end[1:2, :]).astype(F32) * unit
    return symmetric(blocks[0], blocks[1], diag), square(blocks[2:])


def hand_out(full_ref, a, order, shared_ref, cross_ref, rows_ref):
    d0, off, d1 = [
        full_ref[at_block(order[i]), at_block(order[j])] for i, j in ((0, 0), (0, 1), (1, 1))
    ]
    cross = [full_ref[at_block(order[i]), at_block(order[j])] for i, j in CROSS]
    shared_ref[...] = square((d0, off, off.T, d1))
    cross_ref[...] = square(cross)
    mine = jnp.where(a == 1, order[3], order[2])
    for k in range(2):
        rows_ref[:, k * B : (k + 1) * B] = full_ref[at_block(mine), at_block(order[2 + k])]
    return [paired(d0, d1), off] + cross, [diagonal(d0), diagonal(d1)]


def pair_at(rows, at):
    here = lax.broadcasted_iota(jnp.int32, rows.shape, 1) == at
    held = jnp.where(here, rows.astype(F32), 0.0)
    return [jnp.sum(held[k : k + 1, :]).astype(jnp.int32) for k in range(2)]


def pack_kernel(
    axes, prow, pcol, one, two, k_hbm, m_hbm,
    out_ref, fact_ref, row_gap_ref, col_gap_ref, held_ref, sems,
):
    row, col = lax.axis_index(axes[0]), lax.axis_index(axes[1])
    mate, col_mate = prow[row], pcol[col]
    row_gap_ref[0] = (row ^ mate) - 1
    col_gap_ref[0] = (col ^ col_mate) - 1
    h0, h1 = pair_at(one[0], row)
    order = (h0, h1) + others(h0, h1)
    copies = []
    for which, source in enumerate((k_hbm, m_hbm)):
        targets = [(held_ref.at[which, k], k, k) for k in range(4)]
        for at, (i, j) in ((1, SHARED), (7, OUTER), *((2 + k, pair) for k, pair in enumerate(CROSS))):
            targets.append((out_ref.at[which, at * B : (at + 1) * B, :], i, j))
        for target, i, j in targets:
            copies.append(
                pltpu.make_async_copy(
                    source.at[at_block(order[i]), at_block(order[j])], target, sems.at[len(copies)]
                )
            )
            copies[-1].start()
    g0, g1 = pair_at(two[jnp.minimum(row, mate)], col)
    known = [(row > mate).astype(jnp.int32), (col > col_mate).astype(jnp.int32), *order]
    known += [g0, g1, *others(g0, g1)]
    for k, fact in enumerate(known):
        fact_ref[k] = fact
    for copy in copies:
        copy.wait()
    for which in range(2):
        s0, s1, o0, o1 = [held_ref[which, k].astype(F32) for k in range(4)]
        out_ref[which, :B, :] = paired(s0, s1).astype(BF)
        out_ref[which, 6 * B : 7 * B, :] = paired(o0, o1).astype(BF)
        out_ref[which, 8 * B :, :] = tail_rows([diagonal(s1), diagonal(o1)]).astype(BF)


def one_kernel(
    fact_ref, own, mate,
    x1_ref, code_ref, k_shared, k_cross, k_rows, m_shared, m_cross, m_rows,
    r_ref, x_ref, j_ref, full_ref,
):
    a, _, _, order = facts(fact_ref)
    second = a == 1
    own_k, mate_k, own_m, mate_m = own.at[0], mate.at[0], own.at[1], mate.at[1]
    ks = raw_shared(own_k) + raw_shared(mate_k)
    c = ordered(second, raw_cross(own_k), raw_cross(mate_k))
    x = solve(ks, c, [c.astype(BF)], r_ref, x_ref, j_ref)
    x1_ref[...] = x
    xp = pieces(x, 3)
    full_ref[...] = outer_diag(second, own_k, mate_k) - mm([c.T.astype(BF)], xp, 2)
    blocks, diags = hand_out(full_ref, a, order, k_shared, k_cross, k_rows)
    diags += [diagonal(full_ref[at_block(order[k]), at_block(order[k])]) for k in (2, 3)]
    encode_stiff(blocks, diags, code_ref.at[:K_CODE_ROWS])

    xp = pieces(x, 2)
    ms = raw_shared(own_m) + raw_shared(mate_m)
    d = ordered(second, raw_cross(own_m), raw_cross(mate_m))
    w = mm(pieces(ms, 2), xp, 1) - d
    full_ref[...] = (
        outer_diag(second, own_m, mate_m)
        + mm(pieces(x.T, 2), pieces(w, 2), 1)
        - mm([d.T.astype(BF)], xp, 1)
    )
    blocks, diags = hand_out(full_ref, a, order, m_shared, m_cross, m_rows)
    encode_mass(blocks, diags[1], code_ref.at[K_CODE_ROWS:])


def set_in(second, part):
    zero = jnp.zeros_like(part)
    return jnp.concatenate([jnp.where(second, zero, part), jnp.where(second, part, zero)], axis=1)


def two_kernel(
    fact_ref, mate, x1_ref, k_shared, k_cross, k_rows, m_shared, m_cross, m_rows,
    stiff_ref, mass_ref, basis_ref, r_ref, x_ref, j_ref, spread_ref, x2_ref,
):
    a, b, order_one, order_two = facts(fact_ref)
    second = b == 1
    mate_shared, mate_cross = decode_stiff(mate.at[:K_CODE_ROWS])
    ks = k_shared[...] + mate_shared
    c = ordered(second, k_cross[...], mate_cross)
    x = solve(ks, c, pieces(c, 2), r_ref, x_ref, j_ref)
    x2_ref[...] = x
    xp = pieces(x, 2)
    c_mine = k_cross[:, at_block(a)]
    stiff_ref[...] = set_in(second, k_rows[...]) - mm(pieces(c_mine.T, 2), xp, 1)

    mate_shared, mate_cross = decode_mass(mate.at[K_CODE_ROWS:])
    ms = m_shared[...] + mate_shared
    d = ordered(second, m_cross[...], mate_cross)
    w = mm(pieces(ms, 2), xp, 1) - d
    x_mine = x2_ref[:, at_block(2 * b + a)]
    d_mine = m_cross[:, at_block(a)]
    mass_ref[...] = (
        set_in(second, m_rows[...])
        + mm(pieces(x_mine.T, 2), pieces(w, 2), 1)
        - mm(pieces(d_mine.T, 2), xp, 1)
    )

    eye = identity(B)
    zero = jnp.zeros((B, B), F32)
    for k in range(2):
        spread_ref[at_block(order_two[k]), :] = -x[k * B : (k + 1) * B, :]
        half = jnp.concatenate([eye if k == 0 else zero, eye if k == 1 else zero], axis=1)
        spread_ref[at_block(order_two[2 + k]), :] = set_in(second, half)
    for k in range(2):
        basis_ref[at_block(order_one[2 + k]), :] = spread_ref[at_block(2 * a + k), :]
    x1_sh = jnp.concatenate([x1_ref[:, at_block(order_two[k])] for k in range(2)], axis=1)
    x1_out = jnp.concatenate([x1_ref[:, at_block(order_two[2 + k])] for k in range(2)], axis=1)
    shared = mm(pieces(x1_sh, 2), xp, 1) - set_in(second, x1_out)
    for k in range(2):
        basis_ref[at_block(order_one[k]), :] = shared[k * B : (k + 1) * B, :]


def call(kernel, outs, scratch, known, arrays):
    return pl.pallas_call(
        kernel,
        out_shape=[jax.ShapeDtypeStruct(shape, dtype) for shape, dtype in outs],
        in_specs=[SMEM] + [VMEM] * len(arrays),
        out_specs=[VMEM] * len(outs),
        scratch_shapes=[pltpu.VMEM(shape, F32) for shape in scratch],
        compiler_params=PARAMS,
        cost_estimate=pl.CostEstimate(flops=6 << 30, bytes_accessed=1 << 22, transcendentals=0),
    )(known, *arrays)


def swap(axis, size, gap, array):
    def branch(apart):
        return lambda y: lax.ppermute(y, axis, [(i, i ^ apart) for i in range(size)])

    return lax.switch(gap, [branch(apart) for apart in range(1, size)], array)


def local(stiff, mass, partner_row, partner_col, shared_one, shared_two):
    iface = stiff.shape[0]
    half = iface // 2
    square_half = (half, half)

    packed, known, row_gap, col_gap = pl.pallas_call(
        functools.partial(pack_kernel, ("row", "col")),
        out_shape=[
            jax.ShapeDtypeStruct((2, RAW_ROWS, B), BF),
            jax.ShapeDtypeStruct((FACTS,), jnp.int32),
            jax.ShapeDtypeStruct((1,), jnp.int32),
            jax.ShapeDtypeStruct((1,), jnp.int32),
        ],
        in_specs=[SMEM, SMEM, VMEM, VMEM] + [pl.BlockSpec(memory_space=pltpu.HBM)] * 2,
        out_specs=[VMEM, SMEM, SMEM, SMEM],
        scratch_shapes=[pltpu.VMEM((2, 4, B, B), BF), pltpu.SemaphoreType.DMA((20,))],
        compiler_params=pltpu.CompilerParams(vmem_limit_bytes=60 * 1024 * 1024),
    )(
        partner_row, partner_col,
        jnp.transpose(shared_one, (1, 2, 0)), jnp.transpose(shared_two, (0, 2, 1)), stiff, mass,
    )
    mate = swap("row", partner_row.shape[0], row_gap.reshape(()), packed)
    x1, code, *kept = call(
        one_kernel,
        [((half, iface), F32), ((K_CODE_ROWS + M_CODE_ROWS, B), jnp.int16)]
        + [(square_half, F32), (square_half, F32), ((B, half), F32)] * 2,
        [square_half] * 3 + [(iface, iface)],
        known, (packed, mate),
    )
    mate_code = swap("col", partner_col.shape[0], col_gap.reshape(()), code)
    return tuple(
        call(
            two_kernel,
            [((B, iface), F32), ((B, iface), F32), ((iface, iface), F32)],
            [square_half] * 3 + [(iface, iface), (half, iface)],
            known, (mate_code, x1, *kept),
        )
    )


def solution(mesh):
    return jax.shard_map(
        local,
        mesh=mesh,
        in_specs=(P("row", "col"), P("row", "col"), P(), P(), P(None, "col", None), P()),
        out_specs=(P("row", "col"), P("row", "col"), P("row", "col")),
        check_vma=False,
    )
```

```python
import functools

import jax
import jax.numpy as jnp
from jax import lax
from jax.experimental import pallas as pl
from jax.experimental.pallas import tpu as pltpu
from jax.sharding import PartitionSpec as P

B = 128
BF = jnp.bfloat16
F32 = jnp.float32
LEVEL_ONE = (160.0, 6, 2e-3)
LEVEL_TWO = (64.0, 5, 8e-3)
MOST_STEPS = 40

VMEM = pl.BlockSpec(memory_space=pltpu.VMEM)
SMEM = pl.BlockSpec(memory_space=pltpu.SMEM)
HBM = pl.BlockSpec(memory_space=pltpu.HBM)
PARAMS = pltpu.CompilerParams(vmem_limit_bytes=40 * 1024 * 1024)

SHARED, OUTER = (0, 1), (2, 3)
CROSS = ((0, 2), (0, 3), (1, 2), (1, 3))
TAIL = 16
RAW_ROWS = 8 * B + TAIL
CODED = 6
HIGH_ROWS = CODED * B
LOW_ROWS = CODED * B // 4
CODE_ROWS = HIGH_ROWS + LOW_ROWS + TAIL
CODE_BITS = 19
LOW_QUADS = (((0, 0, B), (1, 0, B), (2, 0, B), (3, 0, B)), ((4, 0, B // 2), (4, B // 2, B), (5, 0, B // 2), (5, B // 2, B)))
SECOND_ROW, SECOND_COL, ORDER_ONE, ORDER_TWO, FACTS = 0, 1, 2, 6, 10


def pieces(x, count):
    out = []
    for _ in range(count - 1):
        top = x.astype(BF)
        out.append(top)
        x = x - top.astype(F32)
    out.append(x.astype(BF))
    return out


def mm(left, right, order):
    total = None
    for level in range(order, -1, -1):
        for i in range(len(left)):
            j = level - i
            if 0 <= j < len(right):
                term = jnp.dot(left[i], right[j], preferred_element_type=F32)
                total = term if total is None else total + term
    return total


def identity(n):
    return (
        lax.broadcasted_iota(jnp.int32, (n, n), 0) == lax.broadcasted_iota(jnp.int32, (n, n), 1)
    ).astype(F32)


def row_norm(x):
    return jnp.max(jnp.sum(jnp.abs(x), axis=0, keepdims=True), axis=1, keepdims=True)


def solve(level, a, c, c_pieces, r_ref, x_ref, j_ref):
    ratio, steps, goal = level
    n = a.shape[0]
    eye = identity(n)
    picked = a * eye
    down = lax.rsqrt(jnp.sum(picked, axis=1, keepdims=True))
    across = lax.rsqrt(jnp.sum(picked, axis=0, keepdims=True))
    scaled = a * down * across
    j_ref[...] = scaled
    alpha = 2.0 / (row_norm(scaled) * (1.0 + 1.0 / ratio))
    r_ref[...] = eye - alpha * scaled
    x_ref[...] = alpha * eye

    def step(_, t):
        r, x = r_ref[...], x_ref[...]
        rp, xp = pieces(r, 2), pieces(x, 2)
        stacked = [jnp.concatenate([rp[k], xp[k]], axis=0) for k in range(2)]
        prod = mm(stacked, rp, 1)
        t_next = 2.0 * t * t - 1.0
        extra = 1.0 / t_next
        r_ref[...] = prod[:n] * (1.0 + extra) - extra * eye
        x_ref[...] = (x + prod[n:]) * (1.0 + extra)
        return t_next

    first = (ratio + 1.0) / (ratio - 1.0)
    lax.fori_loop(0, steps, step, jnp.full((1, 1), first, F32))

    def unfinished(state):
        count, norm = state
        return (norm > goal) & (count < MOST_STEPS)

    def newton(state):
        count, _ = state
        x = x_ref[...]
        xp = pieces(x, 3)
        r = eye - mm(pieces(j_ref[...], 3), xp, 2)
        x_ref[...] = x + mm(xp, pieces(r, 3), 2)
        norm = jnp.max(row_norm(r))
        return count + 1, jnp.where(norm < 1.0, norm * norm, norm)

    lax.while_loop(unfinished, newton, (jnp.int32(0), jnp.max(row_norm(r_ref[...]))))

    inverse = pieces(x_ref[...] * down * across, 2)
    y = mm(inverse, c_pieces, 1)
    rest = c - mm(pieces(a, 3), pieces(y, 3), 2)
    return y + mm(inverse, pieces(rest, 2), 1)


def others(h0, h1):
    def has(k):
        return (h0 == k) | (h1 == k)

    low = jnp.where(has(0), jnp.where(has(1), 2, 1), 0)
    return low, 6 - h0 - h1 - low


def facts(ref):
    order_one = [ref[ORDER_ONE + k] for k in range(4)]
    order_two = [ref[ORDER_TWO + k] for k in range(4)]
    return ref[SECOND_ROW], ref[SECOND_COL], order_one, order_two


def at_block(k):
    return pl.ds(pl.multiple_of(k * B, B), B)


def triangles():
    rows = lax.broadcasted_iota(jnp.int32, (B, B), 0)
    cols = lax.broadcasted_iota(jnp.int32, (B, B), 1)
    return rows, cols


def paired(first, second):
    rows, cols = triangles()
    return jnp.where(rows >= cols, first, second)


def diagonal(block):
    rows, cols = triangles()
    return jnp.sum(jnp.where(rows == cols, block, 0.0), axis=0, keepdims=True)


def unpaired(pair, diag):
    rows, cols = triangles()
    turned = pair.T
    first = jnp.where(rows >= cols, pair, turned)
    second = jnp.where(rows == cols, diag, jnp.where(rows < cols, pair, turned))
    return first, second


def symmetric(pair, off, diag):
    d0, d1 = unpaired(pair, diag)
    return square((d0, off, off.T, d1))


def square(blocks):
    w, x, y, z = blocks
    return jnp.concatenate(
        [jnp.concatenate([w, x], axis=1), jnp.concatenate([y, z], axis=1)], axis=0
    )


def block(ref, k):
    return ref[k * B : (k + 1) * B, :].astype(F32)


def tail(ref, start, k):
    return ref[start : start + TAIL, :].astype(F32)[k : k + 1, :]


def raw_shared(ref):
    return symmetric(block(ref, 0), block(ref, 1), tail(ref, 8 * B, 0))


def raw_cross(ref):
    return square([block(ref, 2 + k) for k in range(4)])


def raw_outer(ref):
    return symmetric(block(ref, 6), block(ref, 7), tail(ref, 8 * B, 1))


def ordered(second, own, mate):
    return jnp.concatenate([jnp.where(second, mate, own), jnp.where(second, own, mate)], axis=1)


def outer_diag(second, own_ref, mate_ref):
    own, mate = raw_outer(own_ref), raw_outer(mate_ref)
    zero = jnp.zeros((2 * B, 2 * B), F32)
    top = jnp.concatenate([jnp.where(second, mate, own), zero], axis=1)
    bottom = jnp.concatenate([zero, jnp.where(second, own, mate)], axis=1)
    return jnp.concatenate([top, bottom], axis=0)


def tail_rows(rows):
    at = lax.broadcasted_iota(jnp.int32, (TAIL, B), 0)
    out = jnp.zeros((TAIL, B), rows[0].dtype)
    for k, row in enumerate(rows):
        out = jnp.where(at == k, row, out)
    return out


def whole(x, scale):
    limit = 2.0**CODE_BITS - 1.0
    return jnp.clip(jnp.floor(x * scale + 0.5), -limit, limit).astype(jnp.int32)


def store_code(numbers, row, exponents, ref):
    for k, number in enumerate(numbers):
        ref[k * B : (k + 1) * B, :] = (number >> 4).astype(jnp.int16)
    at = HIGH_ROWS
    for quad in LOW_QUADS:
        w, x, y, z = [numbers[k][start:stop] & 15 for k, start, stop in quad]
        packed = ((w * 16 + x) * 16 + y) * 16 + z - 32768
        ref[at : at + packed.shape[0], :] = packed.astype(jnp.int16)
        at += packed.shape[0]
    rows = [row >> 4, row & 15] + [e.astype(jnp.int32) for e in exponents]
    ref[CODE_ROWS - TAIL : CODE_ROWS, :] = tail_rows(rows).astype(jnp.int16)


def load_code(ref):
    end = ref[CODE_ROWS - TAIL : CODE_ROWS, :].astype(jnp.int32)
    first = ref[HIGH_ROWS : HIGH_ROWS + B, :].astype(jnp.int32) + 32768
    rest = ref[HIGH_ROWS + B : HIGH_ROWS + LOW_ROWS, :].astype(jnp.int32) + 32768
    lows = [(first >> shift) & 15 for shift in (12, 8, 4, 0)]
    halves = [(rest >> shift) & 15 for shift in (12, 8, 4, 0)]
    lows += [jnp.concatenate(halves[k : k + 2], axis=0) for k in (0, 2)]
    numbers = [
        (ref[k * B : (k + 1) * B, :].astype(jnp.int32) * 16 + lows[k]).astype(F32)
        for k in range(CODED)
    ]
    row = (end[0:1, :] * 16 + end[1:2, :]).astype(F32)
    return numbers, row, [end[2 + k : 3 + k, :].astype(F32) for k in range(4)]


def upright(row):
    rows, cols = triangles()
    return jnp.sum(jnp.where(rows == cols, row, 0.0), axis=1, keepdims=True)


def stiff_units(exponents, sign, size):
    across = [jnp.exp2(sign * e) for e in exponents]
    down = [upright(across[k]) * size for k in range(2)]
    units = [paired(down[0] * across[0], down[1] * across[1]), down[0] * across[1]]
    units += [down[i] * across[j] for i, j in CROSS]
    return units, across[1] * across[1] * size


def encode_stiff(blocks, diags, ref):
    exponents = [jnp.ceil(0.5 * jnp.log2(jnp.clip(d, 1e-30, 1e30)) + 2e-3) for d in diags]
    units, unit = stiff_units(exponents, -1.0, 2.0**CODE_BITS)
    numbers = [whole(x, scale) for x, scale in zip(blocks, units)]
    store_code(numbers, whole(diags[1], unit), exponents, ref)


def decode_stiff(ref):
    numbers, row, exponents = load_code(ref)
    units, unit = stiff_units(exponents, 1.0, 2.0**-CODE_BITS)
    blocks = [x * scale for x, scale in zip(numbers, units)]
    return symmetric(blocks[0], blocks[1], row * unit), square(blocks[2:])


def encode_mass(blocks, diag, ref):
    largest = jnp.max(jnp.abs(diag), axis=1, keepdims=True)
    for x in blocks:
        top = jnp.max(jnp.max(jnp.abs(x), axis=0, keepdims=True), axis=1, keepdims=True)
        largest = jnp.maximum(largest, top)
    power = jnp.ceil(jnp.log2(jnp.clip(largest, 1e-30, 1e30)) + 2e-3)
    scale = jnp.exp2(CODE_BITS - power)
    exponent = jnp.zeros((1, B), F32) + power
    store_code([whole(x, scale) for x in blocks], whole(diag, scale), [exponent], ref)


def decode_mass(ref):
    numbers, row, exponents = load_code(ref)
    unit = jnp.exp2(exponents[0][:, 0:1] - CODE_BITS)
    blocks = [x * unit for x in numbers]
    return symmetric(blocks[0], blocks[1], row * unit), square(blocks[2:])


def hand_out(full_ref, a, order, shared_ref, cross_ref, rows_ref):
    d0, off, d1 = [
        full_ref[at_block(order[i]), at_block(order[j])] for i, j in ((0, 0), (0, 1), (1, 1))
    ]
    cross = [full_ref[at_block(order[i]), at_block(order[j])] for i, j in CROSS]
    shared_ref[...] = square((d0, off, off.T, d1))
    cross_ref[...] = square(cross)
    mine = jnp.where(a == 1, order[3], order[2])
    for k in range(2):
        rows_ref[:, k * B : (k + 1) * B] = full_ref[at_block(mine), at_block(order[2 + k])]
    return [paired(d0, d1), off] + cross, [diagonal(d0), diagonal(d1)]


def pair_at(rows, at):
    here = lax.broadcasted_iota(jnp.int32, rows.shape, 1) == at
    held = jnp.where(here, rows.astype(F32), 0.0)
    return [jnp.sum(held[k : k + 1, :]).astype(jnp.int32) for k in range(2)]


def start(copies):
    for copy in copies:
        copy.start()
    return copies


def finish(copies):
    for copy in copies:
        copy.wait()


def pack_kernel(
    axes, prow_hbm, pcol_hbm, one_hbm, two_hbm, k_hbm, m_hbm,
    out_ref, fact_ref, row_gap_ref, col_gap_ref, prow, pcol, one, two, k_ref, m_ref, sems,
):
    pairs = (
        (prow_hbm, prow), (pcol_hbm, pcol), (one_hbm, one), (two_hbm, two), (k_hbm, k_ref), (m_hbm, m_ref)
    )
    copies = start(
        [pltpu.make_async_copy(a, b, sems.at[k]) for k, (a, b) in enumerate(pairs)]
    )
    row, col = lax.axis_index(axes[0]), lax.axis_index(axes[1])
    finish(copies[:4])
    mate, col_mate = prow[row], pcol[col]
    row_gap_ref[0] = (row ^ mate) - 1
    col_gap_ref[0] = (col ^ col_mate) - 1
    h0, h1 = pair_at(one[0], row)
    g0, g1 = pair_at(two[jnp.minimum(row, mate)], col)
    order = (h0, h1) + others(h0, h1)
    known = [(row > mate).astype(jnp.int32), (col > col_mate).astype(jnp.int32), *order]
    known += [g0, g1, *others(g0, g1)]
    for k, fact in enumerate(known):
        fact_ref[k] = fact
    for which, ref in enumerate((k_ref, m_ref)):
        finish([copies[4 + which]])
        for at, (i, j) in ((1, SHARED), (7, OUTER), *((2 + k, pair) for k, pair in enumerate(CROSS))):
            out_ref[which, at * B : (at + 1) * B, :] = ref[at_block(order[i]), at_block(order[j])]
        s0, s1, o0, o1 = [ref[at_block(k), at_block(k)].astype(F32) for k in order]
        out_ref[which, :B, :] = paired(s0, s1).astype(BF)
        out_ref[which, 6 * B : 7 * B, :] = paired(o0, o1).astype(BF)
        out_ref[which, 8 * B :, :] = tail_rows([diagonal(s1), diagonal(o1)]).astype(BF)


def one_kernel(
    fact_ref, own, mate,
    x1_ref, code_ref, k_shared, k_cross, k_rows, m_shared, m_cross, m_rows,
    r_ref, x_ref, j_ref, full_k, full_m,
):
    a, _, _, order = facts(fact_ref)
    second = a == 1
    own_k, mate_k, own_m, mate_m = own.at[0], mate.at[0], own.at[1], mate.at[1]
    ks = raw_shared(own_k) + raw_shared(mate_k)
    c = ordered(second, raw_cross(own_k), raw_cross(mate_k))
    x = solve(LEVEL_ONE, ks, c, [c.astype(BF)], r_ref, x_ref, j_ref)
    x1_ref[...] = x
    full_k[...] = outer_diag(second, own_k, mate_k) - mm([c.T.astype(BF)], pieces(x, 3), 2)
    xp = pieces(x, 2)
    ms = raw_shared(own_m) + raw_shared(mate_m)
    d = ordered(second, raw_cross(own_m), raw_cross(mate_m))
    w = mm(pieces(ms, 2), xp, 1) - d
    full_m[...] = (
        outer_diag(second, own_m, mate_m)
        + mm(pieces(x.T, 2), pieces(w, 2), 1)
        - mm([d.T.astype(BF)], xp, 1)
    )
    blocks, diags = hand_out(full_k, a, order, k_shared, k_cross, k_rows)
    diags += [diagonal(full_k[at_block(order[k]), at_block(order[k])]) for k in (2, 3)]
    encode_stiff(blocks, diags, code_ref.at[0])
    blocks, diags = hand_out(full_m, a, order, m_shared, m_cross, m_rows)
    encode_mass(blocks, diags[1], code_ref.at[1])


def set_in(second, part):
    zero = jnp.zeros_like(part)
    return jnp.concatenate([jnp.where(second, zero, part), jnp.where(second, part, zero)], axis=1)


def two_kernel(
    fact_ref, mate, x1_ref, k_shared, k_cross, k_rows, m_shared, m_cross, m_rows,
    stiff_ref, mass_ref, basis_ref, r_ref, x_ref, j_ref, spread_ref, x2_ref,
):
    a, b, order_one, order_two = facts(fact_ref)
    second = b == 1
    mate_shared, mate_cross = decode_stiff(mate.at[0])
    ks = k_shared[...] + mate_shared
    c = ordered(second, k_cross[...], mate_cross)
    x = solve(LEVEL_TWO, ks, c, pieces(c, 2), r_ref, x_ref, j_ref)
    x2_ref[...] = x
    xp = pieces(x, 2)
    c_mine = k_cross[:, at_block(a)]
    stiff_ref[...] = set_in(second, k_rows[...]) - mm(pieces(c_mine.T, 2), xp, 1)

    mate_shared, mate_cross = decode_mass(mate.at[1])
    ms = m_shared[...] + mate_shared
    d = ordered(second, m_cross[...], mate_cross)
    w = mm(pieces(ms, 2), xp, 1) - d
    x_mine = x2_ref[:, at_block(2 * b + a)]
    d_mine = m_cross[:, at_block(a)]
    mass_ref[...] = (
        set_in(second, m_rows[...])
        + mm(pieces(x_mine.T, 2), pieces(w, 2), 1)
        - mm(pieces(d_mine.T, 2), xp, 1)
    )

    eye = identity(B)
    zero = jnp.zeros((B, B), F32)
    for k in range(2):
        spread_ref[at_block(order_two[k]), :] = -x[k * B : (k + 1) * B, :]
        half = jnp.concatenate([eye if k == 0 else zero, eye if k == 1 else zero], axis=1)
        spread_ref[at_block(order_two[2 + k]), :] = set_in(second, half)
    for k in range(2):
        basis_ref[at_block(order_one[2 + k]), :] = spread_ref[at_block(2 * a + k), :]
    x1_sh = jnp.concatenate([x1_ref[:, at_block(order_two[k])] for k in range(2)], axis=1)
    x1_out = jnp.concatenate([x1_ref[:, at_block(order_two[2 + k])] for k in range(2)], axis=1)
    shared = mm(pieces(x1_sh, 2), xp, 1) - set_in(second, x1_out)
    for k in range(2):
        basis_ref[at_block(order_one[k]), :] = shared[k * B : (k + 1) * B, :]


def call(kernel, outs, scratch, known, arrays):
    return pl.pallas_call(
        kernel,
        out_shape=[jax.ShapeDtypeStruct(shape, dtype) for shape, dtype in outs],
        in_specs=[SMEM] + [VMEM] * len(arrays),
        out_specs=[VMEM] * len(outs),
        scratch_shapes=[pltpu.VMEM(shape, dtype) for shape, dtype in scratch],
        compiler_params=PARAMS,
        cost_estimate=pl.CostEstimate(flops=6 << 30, bytes_accessed=1 << 22, transcendentals=0),
    )(known, *arrays)


def swap(axis, size, gap, array):
    def branch(apart):
        return lambda y: lax.ppermute(y, axis, [(i, i ^ apart) for i in range(size)])

    return lax.switch(gap, [branch(apart) for apart in range(1, size)], array)


def local(stiff, mass, partner_row, partner_col, shared_one, shared_two):
    iface = stiff.shape[0]
    half = iface // 2
    square_half = ((half, half), F32)
    n_row, n_col = partner_row.shape[0], partner_col.shape[0]
    raw = ((2, RAW_ROWS, B), BF)
    code = ((2, CODE_ROWS, B), jnp.int16)

    packed, known, row_gap, col_gap = pl.pallas_call(
        functools.partial(pack_kernel, ("row", "col")),
        out_shape=[
            jax.ShapeDtypeStruct(*raw),
            jax.ShapeDtypeStruct((FACTS,), jnp.int32),
            jax.ShapeDtypeStruct((1,), jnp.int32),
            jax.ShapeDtypeStruct((1,), jnp.int32),
        ],
        in_specs=[HBM] * 6,
        out_specs=[VMEM, SMEM, SMEM, SMEM],
        scratch_shapes=[
            pltpu.SMEM((n_row,), jnp.int32),
            pltpu.SMEM((n_col,), jnp.int32),
            pltpu.VMEM((1, 2, n_row), jnp.int32),
            pltpu.VMEM((n_row, 2, n_col), jnp.int32),
            pltpu.VMEM(stiff.shape, BF),
            pltpu.VMEM(mass.shape, BF),
            pltpu.SemaphoreType.DMA((6,)),
        ],
        compiler_params=pltpu.CompilerParams(vmem_limit_bytes=60 * 1024 * 1024),
    )(
        partner_row, partner_col,
        jnp.transpose(shared_one, (1, 2, 0)), jnp.transpose(shared_two, (0, 2, 1)), stiff, mass,
    )
    mate = swap("row", n_row, row_gap.reshape(()), packed)
    x1, codes, *kept = call(
        one_kernel,
        [((half, iface), F32), code] + [square_half, square_half, ((B, half), F32)] * 2,
        [square_half] * 3 + [((iface, iface), F32)] * 2,
        known, (packed, mate),
    )
    mate_codes = swap("col", n_col, col_gap.reshape(()), codes)
    return tuple(
        call(
            two_kernel,
            [((B, iface), F32), ((B, iface), F32), ((iface, iface), F32)],
            [square_half] * 3 + [((iface, iface), F32), ((half, iface), F32)],
            known, (mate_codes, x1, *kept),
        )
    )


def solution(mesh):
    return jax.shard_map(
        local,
        mesh=mesh,
        in_specs=(P("row", "col"), P("row", "col"), P(), P(), P(None, "col", None), P()),
        out_specs=(P("row", "col"), P("row", "col"), P("row", "col")),
        check_vma=False,
    )
```

```python
import functools

import jax
import jax.numpy as jnp
from jax import lax
from jax.experimental import pallas as pl
from jax.experimental.pallas import tpu as pltpu
from jax.sharding import PartitionSpec as P

B = 128
BF = jnp.bfloat16
F32 = jnp.float32
LEVEL_ONE = (160.0, 6, 2e-3)
LEVEL_TWO = (64.0, 5, 8e-3)
MOST_STEPS = 40

VMEM = pl.BlockSpec(memory_space=pltpu.VMEM)
SMEM = pl.BlockSpec(memory_space=pltpu.SMEM)
HBM = pl.BlockSpec(memory_space=pltpu.HBM)
PARAMS = pltpu.CompilerParams(vmem_limit_bytes=40 * 1024 * 1024)

SHARED, OUTER = (0, 1), (2, 3)
CROSS = ((0, 2), (0, 3), (1, 2), (1, 3))
TAIL = 16
RAW_ROWS = 8 * B + TAIL
CODED = 6
HIGH_ROWS = CODED * B
LOW_ROWS = CODED * B // 4
CODE_ROWS = HIGH_ROWS + LOW_ROWS + TAIL
CODE_BITS = 19
LOW_QUADS = (((0, 0, B), (1, 0, B), (2, 0, B), (3, 0, B)), ((4, 0, B // 2), (4, B // 2, B), (5, 0, B // 2), (5, B // 2, B)))
SECOND_ROW, SECOND_COL, ORDER_ONE, ORDER_TWO, FACTS = 0, 1, 2, 6, 10


def pieces(x, count):
    out = []
    for _ in range(count - 1):
        top = x.astype(BF)
        out.append(top)
        x = x - top.astype(F32)
    out.append(x.astype(BF))
    return out


def mm(left, right, order):
    total = None
    for level in range(order, -1, -1):
        for i in range(len(left)):
            j = level - i
            if 0 <= j < len(right):
                term = jnp.dot(left[i], right[j], preferred_element_type=F32)
                total = term if total is None else total + term
    return total


def identity(n):
    return (
        lax.broadcasted_iota(jnp.int32, (n, n), 0) == lax.broadcasted_iota(jnp.int32, (n, n), 1)
    ).astype(F32)


def row_norm(x):
    return jnp.max(jnp.sum(jnp.abs(x), axis=0, keepdims=True), axis=1, keepdims=True)


def solve(level, a, c, c_pieces, r_ref, x_ref, j_ref):
    ratio, steps, goal = level
    n = a.shape[0]
    eye = identity(n)
    picked = a * eye
    down = lax.rsqrt(jnp.sum(picked, axis=1, keepdims=True))
    across = lax.rsqrt(jnp.sum(picked, axis=0, keepdims=True))
    scaled = a * down * across
    j_ref[...] = scaled
    alpha = 2.0 / (row_norm(scaled) * (1.0 + 1.0 / ratio))
    r_ref[...] = eye - alpha * scaled
    x_ref[...] = alpha * eye

    def step(_, t):
        r, x = r_ref[...], x_ref[...]
        rp, xp = pieces(r, 2), pieces(x, 2)
        stacked = [jnp.concatenate([rp[k], xp[k]], axis=0) for k in range(2)]
        prod = mm(stacked, rp, 1)
        t_next = 2.0 * t * t - 1.0
        extra = 1.0 / t_next
        r_ref[...] = prod[:n] * (1.0 + extra) - extra * eye
        x_ref[...] = (x + prod[n:]) * (1.0 + extra)
        return t_next

    first = (ratio + 1.0) / (ratio - 1.0)
    lax.fori_loop(0, steps, step, jnp.full((1, 1), first, F32))

    def unfinished(state):
        count, norm = state
        return (norm > goal) & (count < MOST_STEPS)

    def newton(state):
        count, _ = state
        x = x_ref[...]
        xp = pieces(x, 3)
        r = eye - mm(pieces(j_ref[...], 3), xp, 2)
        x_ref[...] = x + mm(xp, pieces(r, 3), 2)
        norm = jnp.max(row_norm(r))
        return count + 1, jnp.where(norm < 1.0, norm * norm, norm)

    lax.while_loop(unfinished, newton, (jnp.int32(0), jnp.max(row_norm(r_ref[...]))))

    inverse = pieces(x_ref[...] * down * across, 2)
    y = mm(inverse, c_pieces, 1)
    rest = c - mm(pieces(a, 3), pieces(y, 3), 2)
    return y + mm(inverse[:1], pieces(rest, 1), 0)


def others(h0, h1):
    def has(k):
        return (h0 == k) | (h1 == k)

    low = jnp.where(has(0), jnp.where(has(1), 2, 1), 0)
    return low, 6 - h0 - h1 - low


def facts(row, which):
    lanes = lax.broadcasted_iota(jnp.int32, row.shape, 1)
    return [jnp.sum(jnp.where(lanes == k, row, 0.0)).astype(jnp.int32) for k in which]


def at_block(k):
    return pl.ds(pl.multiple_of(k * B, B), B)


def triangles():
    rows = lax.broadcasted_iota(jnp.int32, (B, B), 0)
    cols = lax.broadcasted_iota(jnp.int32, (B, B), 1)
    return rows, cols


def paired(first, second):
    rows, cols = triangles()
    return jnp.where(rows >= cols, first, second)


def diagonal(block):
    rows, cols = triangles()
    return jnp.sum(jnp.where(rows == cols, block, 0.0), axis=0, keepdims=True)


def unpaired(pair, diag):
    rows, cols = triangles()
    turned = pair.T
    first = jnp.where(rows >= cols, pair, turned)
    second = jnp.where(rows == cols, diag, jnp.where(rows < cols, pair, turned))
    return first, second


def symmetric(pair, off, diag):
    d0, d1 = unpaired(pair, diag)
    return square((d0, off, off.T, d1))


def square(blocks):
    w, x, y, z = blocks
    return jnp.concatenate(
        [jnp.concatenate([w, x], axis=1), jnp.concatenate([y, z], axis=1)], axis=0
    )


def block(ref, k):
    return ref[k * B : (k + 1) * B, :].astype(F32)


def tail(ref, start, k):
    return ref[start : start + TAIL, :].astype(F32)[k : k + 1, :]


def raw_shared(ref):
    return symmetric(block(ref, 0), block(ref, 1), tail(ref, 8 * B, 0))


def raw_cross(ref):
    return square([block(ref, 2 + k) for k in range(4)])


def raw_outer(ref):
    return symmetric(block(ref, 6), block(ref, 7), tail(ref, 8 * B, 1))


def ordered(second, own, mate):
    return jnp.concatenate([jnp.where(second, mate, own), jnp.where(second, own, mate)], axis=1)


def outer_diag(second, own_ref, mate_ref):
    own, mate = raw_outer(own_ref), raw_outer(mate_ref)
    zero = jnp.zeros((2 * B, 2 * B), F32)
    top = jnp.concatenate([jnp.where(second, mate, own), zero], axis=1)
    bottom = jnp.concatenate([zero, jnp.where(second, own, mate)], axis=1)
    return jnp.concatenate([top, bottom], axis=0)


def tail_rows(rows):
    at = lax.broadcasted_iota(jnp.int32, (TAIL, B), 0)
    out = jnp.zeros((TAIL, B), rows[0].dtype)
    for k, row in enumerate(rows):
        out = jnp.where(at == k, row, out)
    return out


def whole(x, scale):
    limit = 2.0**CODE_BITS - 1.0
    return jnp.clip(jnp.floor(x * scale + 0.5), -limit, limit).astype(jnp.int32)


def store_code(numbers, row, exponents, ref):
    for k, number in enumerate(numbers):
        ref[k * B : (k + 1) * B, :] = (number >> 4).astype(jnp.int16)
    at = HIGH_ROWS
    for quad in LOW_QUADS:
        w, x, y, z = [numbers[k][start:stop] & 15 for k, start, stop in quad]
        packed = ((w * 16 + x) * 16 + y) * 16 + z - 32768
        ref[at : at + packed.shape[0], :] = packed.astype(jnp.int16)
        at += packed.shape[0]
    rows = [row >> 4, row & 15] + [e.astype(jnp.int32) for e in exponents]
    ref[CODE_ROWS - TAIL : CODE_ROWS, :] = tail_rows(rows).astype(jnp.int16)


def load_code(ref):
    end = ref[CODE_ROWS - TAIL : CODE_ROWS, :].astype(jnp.int32)
    first = ref[HIGH_ROWS : HIGH_ROWS + B, :].astype(jnp.int32) + 32768
    rest = ref[HIGH_ROWS + B : HIGH_ROWS + LOW_ROWS, :].astype(jnp.int32) + 32768
    lows = [(first >> shift) & 15 for shift in (12, 8, 4, 0)]
    halves = [(rest >> shift) & 15 for shift in (12, 8, 4, 0)]
    lows += [jnp.concatenate(halves[k : k + 2], axis=0) for k in (0, 2)]
    numbers = [
        (ref[k * B : (k + 1) * B, :].astype(jnp.int32) * 16 + lows[k]).astype(F32)
        for k in range(CODED)
    ]
    row = (end[0:1, :] * 16 + end[1:2, :]).astype(F32)
    return numbers, row, [end[2 + k : 3 + k, :].astype(F32) for k in range(4)]


def upright(row):
    rows, cols = triangles()
    return jnp.sum(jnp.where(rows == cols, row, 0.0), axis=1, keepdims=True)


def stiff_units(exponents, sign, size):
    across = [jnp.exp2(sign * e) for e in exponents]
    down = [upright(across[k]) * size for k in range(2)]
    units = [paired(down[0] * across[0], down[1] * across[1]), down[0] * across[1]]
    units += [down[i] * across[j] for i, j in CROSS]
    return units, across[1] * across[1] * size


def encode_stiff(blocks, diags, ref):
    exponents = [jnp.ceil(0.5 * jnp.log2(jnp.clip(d, 1e-30, 1e30)) + 2e-3) for d in diags]
    units, unit = stiff_units(exponents, -1.0, 2.0**CODE_BITS)
    numbers = [whole(x, scale) for x, scale in zip(blocks, units)]
    store_code(numbers, whole(diags[1], unit), exponents, ref)


def decode_stiff(ref):
    numbers, row, exponents = load_code(ref)
    units, unit = stiff_units(exponents, 1.0, 2.0**-CODE_BITS)
    blocks = [x * scale for x, scale in zip(numbers, units)]
    return symmetric(blocks[0], blocks[1], row * unit), square(blocks[2:])


def encode_mass(blocks, diag, ref):
    largest = jnp.max(jnp.abs(diag), axis=1, keepdims=True)
    for x in blocks:
        top = jnp.max(jnp.max(jnp.abs(x), axis=0, keepdims=True), axis=1, keepdims=True)
        largest = jnp.maximum(largest, top)
    power = jnp.ceil(jnp.log2(jnp.clip(largest, 1e-30, 1e30)) + 2e-3)
    scale = jnp.exp2(CODE_BITS - power)
    exponent = jnp.zeros((1, B), F32) + power
    store_code([whole(x, scale) for x in blocks], whole(diag, scale), [exponent], ref)


def decode_mass(ref):
    numbers, row, exponents = load_code(ref)
    unit = jnp.exp2(exponents[0][:, 0:1] - CODE_BITS)
    blocks = [x * unit for x in numbers]
    return symmetric(blocks[0], blocks[1], row * unit), square(blocks[2:])


def hand_out(full_ref, a, order, shared_ref, cross_ref, rows_ref):
    d0, off, d1 = [
        full_ref[at_block(order[i]), at_block(order[j])] for i, j in ((0, 0), (0, 1), (1, 1))
    ]
    cross = [full_ref[at_block(order[i]), at_block(order[j])] for i, j in CROSS]
    shared_ref[...] = square((d0, off, off.T, d1))
    cross_ref[...] = square(cross)
    mine = jnp.where(a == 1, order[3], order[2])
    for k in range(2):
        rows_ref[:, k * B : (k + 1) * B] = full_ref[at_block(mine), at_block(order[2 + k])]
    return [paired(d0, d1), off] + cross, [diagonal(d0), diagonal(d1)]


def pair_at(rows, at):
    here = lax.broadcasted_iota(jnp.int32, rows.shape, 1) == at
    held = jnp.where(here, rows.astype(F32), 0.0)
    return [jnp.sum(held[k : k + 1, :]).astype(jnp.int32) for k in range(2)]


def start(copies):
    for copy in copies:
        copy.start()
    return copies


def finish(copies):
    for copy in copies:
        copy.wait()


def pack_kernel(
    axes, prow_hbm, pcol_hbm, one_hbm, two_hbm, k_hbm, m_hbm,
    out_ref, row_gap_ref, col_gap_ref, prow, pcol, one, two, k_ref, m_ref, sems,
):
    pairs = (
        (prow_hbm, prow), (pcol_hbm, pcol), (one_hbm, one), (two_hbm, two), (k_hbm, k_ref), (m_hbm, m_ref)
    )
    copies = start(
        [pltpu.make_async_copy(a, b, sems.at[k]) for k, (a, b) in enumerate(pairs)]
    )
    row, col = lax.axis_index(axes[0]), lax.axis_index(axes[1])
    finish(copies[:4])
    mate, col_mate = prow[row], pcol[col]
    row_gap_ref[0] = (row ^ mate) - 1
    col_gap_ref[0] = (col ^ col_mate) - 1
    h0, h1 = pair_at(one[0], row)
    g0, g1 = pair_at(two[jnp.minimum(row, mate)], col)
    order = (h0, h1) + others(h0, h1)
    known = [(row > mate).astype(jnp.int32), (col > col_mate).astype(jnp.int32), *order]
    known += [g0, g1, *others(g0, g1)]
    lanes = lax.broadcasted_iota(jnp.int32, (1, B), 1)
    noted = jnp.zeros((1, B), F32)
    for k, fact in enumerate(known):
        noted = jnp.where(lanes == k, fact.astype(F32), noted)
    for which, ref in enumerate((k_ref, m_ref)):
        finish([copies[4 + which]])
        for at, (i, j) in ((1, SHARED), (7, OUTER), *((2 + k, pair) for k, pair in enumerate(CROSS))):
            out_ref[which, at * B : (at + 1) * B, :] = ref[at_block(order[i]), at_block(order[j])]
        s0, s1, o0, o1 = [ref[at_block(k), at_block(k)].astype(F32) for k in order]
        out_ref[which, :B, :] = paired(s0, s1).astype(BF)
        out_ref[which, 6 * B : 7 * B, :] = paired(o0, o1).astype(BF)
        out_ref[which, 8 * B :, :] = tail_rows([diagonal(s1), diagonal(o1), noted]).astype(BF)


def one_kernel(
    own, mate,
    fact_ref, x1_ref, code_ref, k_shared, k_cross, k_rows, m_shared, m_cross, m_rows,
    r_ref, x_ref, j_ref, full_k, full_m,
):
    noted = tail(own.at[0], 8 * B, 2)
    fact_ref[...] = jnp.zeros(fact_ref.shape, F32) + noted
    a, *order = facts(noted, (SECOND_ROW, *range(ORDER_TWO, ORDER_TWO + 4)))
    second = noted[:, SECOND_ROW : SECOND_ROW + 1] == 1.0
    own_k, mate_k, own_m, mate_m = own.at[0], mate.at[0], own.at[1], mate.at[1]
    ks = raw_shared(own_k) + raw_shared(mate_k)
    c = ordered(second, raw_cross(own_k), raw_cross(mate_k))
    x = solve(LEVEL_ONE, ks, c, [c.astype(BF)], r_ref, x_ref, j_ref)
    x1_ref[...] = x
    full_k[...] = outer_diag(second, own_k, mate_k) - mm([c.T.astype(BF)], pieces(x, 2), 1)
    xp = pieces(x, 2)
    ms = raw_shared(own_m) + raw_shared(mate_m)
    d = ordered(second, raw_cross(own_m), raw_cross(mate_m))
    w = mm(pieces(ms, 2), xp, 1) - d
    full_m[...] = (
        outer_diag(second, own_m, mate_m)
        + mm(pieces(x.T, 2), pieces(w, 2), 1)
        - mm([d.T.astype(BF)], xp, 1)
    )
    blocks, diags = hand_out(full_k, a, order, k_shared, k_cross, k_rows)
    diags += [diagonal(full_k[at_block(order[k]), at_block(order[k])]) for k in (2, 3)]
    encode_stiff(blocks, diags, code_ref.at[0])
    blocks, diags = hand_out(full_m, a, order, m_shared, m_cross, m_rows)
    encode_mass(blocks, diags[1], code_ref.at[1])


def set_in(second, part):
    zero = jnp.zeros_like(part)
    return jnp.concatenate([jnp.where(second, zero, part), jnp.where(second, part, zero)], axis=1)


def two_kernel(
    fact_ref, mate, x1_ref, k_shared, k_cross, k_rows, m_shared, m_cross, m_rows,
    stiff_ref, mass_ref, basis_ref, r_ref, x_ref, j_ref, spread_ref, x2_ref,
):
    noted = fact_ref[:1, :]
    a, b, *order = facts(noted, range(FACTS))
    order_one, order_two = order[:4], order[4:]
    second = noted[:, SECOND_COL : SECOND_COL + 1] == 1.0
    mate_shared, mate_cross = decode_stiff(mate.at[0])
    ks = k_shared[...] + mate_shared
    c = ordered(second, k_cross[...], mate_cross)
    x = solve(LEVEL_TWO, ks, c, pieces(c, 2), r_ref, x_ref, j_ref)
    x2_ref[...] = x
    xp = pieces(x, 2)
    c_mine = k_cross[:, at_block(a)]
    stiff_ref[...] = set_in(second, k_rows[...]) - mm(pieces(c_mine.T, 2), xp, 1)

    mate_shared, mate_cross = decode_mass(mate.at[1])
    ms = m_shared[...] + mate_shared
    d = ordered(second, m_cross[...], mate_cross)
    w = mm(pieces(ms, 2), xp, 1) - d
    x_mine = x2_ref[:, at_block(2 * b + a)]
    d_mine = m_cross[:, at_block(a)]
    mass_ref[...] = (
        set_in(second, m_rows[...])
        + mm(pieces(x_mine.T, 2), pieces(w, 2), 1)
        - mm(pieces(d_mine.T, 2), xp, 1)
    )

    eye = identity(B)
    zero = jnp.zeros((B, B), F32)
    for k in range(2):
        spread_ref[at_block(order_two[k]), :] = -x[k * B : (k + 1) * B, :]
        half = jnp.concatenate([eye if k == 0 else zero, eye if k == 1 else zero], axis=1)
        spread_ref[at_block(order_two[2 + k]), :] = set_in(second, half)
    for k in range(2):
        basis_ref[at_block(order_one[2 + k]), :] = spread_ref[at_block(2 * a + k), :]
    x1_sh = jnp.concatenate([x1_ref[:, at_block(order_two[k])] for k in range(2)], axis=1)
    x1_out = jnp.concatenate([x1_ref[:, at_block(order_two[2 + k])] for k in range(2)], axis=1)
    shared = mm(pieces(x1_sh, 2), xp, 1) - set_in(second, x1_out)
    for k in range(2):
        basis_ref[at_block(order_one[k]), :] = shared[k * B : (k + 1) * B, :]


def call(kernel, outs, scratch, arrays):
    return pl.pallas_call(
        kernel,
        out_shape=[jax.ShapeDtypeStruct(shape, dtype) for shape, dtype in outs],
        in_specs=[VMEM] * len(arrays),
        out_specs=[VMEM] * len(outs),
        scratch_shapes=[pltpu.VMEM(shape, dtype) for shape, dtype in scratch],
        compiler_params=PARAMS,
        cost_estimate=pl.CostEstimate(flops=6 << 30, bytes_accessed=1 << 22, transcendentals=0),
    )(*arrays)


def swap(axis, size, gap, array):
    def branch(apart):
        return lambda y: lax.ppermute(y, axis, [(i, i ^ apart) for i in range(size)])

    return lax.switch(gap, [branch(apart) for apart in range(1, size)], array)


def local(stiff, mass, partner_row, partner_col, shared_one, shared_two):
    iface = stiff.shape[0]
    half = iface // 2
    square_half = ((half, half), F32)
    n_row, n_col = partner_row.shape[0], partner_col.shape[0]
    raw = ((2, RAW_ROWS, B), BF)
    code = ((2, CODE_ROWS, B), jnp.int16)

    packed, row_gap, col_gap = pl.pallas_call(
        functools.partial(pack_kernel, ("row", "col")),
        out_shape=[
            jax.ShapeDtypeStruct(*raw),
            jax.ShapeDtypeStruct((1,), jnp.int32),
            jax.ShapeDtypeStruct((1,), jnp.int32),
        ],
        in_specs=[HBM] * 6,
        out_specs=[VMEM, SMEM, SMEM],
        scratch_shapes=[
            pltpu.SMEM((n_row,), jnp.int32),
            pltpu.SMEM((n_col,), jnp.int32),
            pltpu.VMEM((1, 2, n_row), jnp.int32),
            pltpu.VMEM((n_row, 2, n_col), jnp.int32),
            pltpu.VMEM(stiff.shape, BF),
            pltpu.VMEM(mass.shape, BF),
            pltpu.SemaphoreType.DMA((6,)),
        ],
        compiler_params=pltpu.CompilerParams(vmem_limit_bytes=60 * 1024 * 1024),
    )(
        partner_row, partner_col,
        jnp.transpose(shared_one, (1, 2, 0)), jnp.transpose(shared_two, (0, 2, 1)), stiff, mass,
    )
    mate = swap("row", n_row, row_gap.reshape(()), packed)
    known, x1, codes, *kept = call(
        one_kernel,
        [((8, B), F32), ((half, iface), F32), code] + [square_half, square_half, ((B, half), F32)] * 2,
        [square_half] * 3 + [((iface, iface), F32)] * 2,
        (packed, mate),
    )
    mate_codes = swap("col", n_col, col_gap.reshape(()), codes)
    return tuple(
        call(
            two_kernel,
            [((B, iface), F32), ((B, iface), F32), ((iface, iface), F32)],
            [square_half] * 3 + [((iface, iface), F32), ((half, iface), F32)],
            (known, mate_codes, x1, *kept),
        )
    )


def solution(mesh):
    return jax.shard_map(
        local,
        mesh=mesh,
        in_specs=(P("row", "col"), P("row", "col"), P(), P(), P(None, "col", None), P()),
        out_specs=(P("row", "col"), P("row", "col"), P("row", "col")),
        check_vma=False,
    )
```

```python
import functools

import jax
import jax.numpy as jnp
from jax import lax
from jax.experimental import pallas as pl
from jax.experimental.pallas import tpu as pltpu
from jax.sharding import PartitionSpec as P

B = 128
BF = jnp.bfloat16
F32 = jnp.float32
LEVEL_ONE = (160.0, 6, 2e-3)
LEVEL_TWO = (64.0, 5, 8e-3)
MOST_STEPS = 40

VMEM = pl.BlockSpec(memory_space=pltpu.VMEM)
SMEM = pl.BlockSpec(memory_space=pltpu.SMEM)
HBM = pl.BlockSpec(memory_space=pltpu.HBM)
PARAMS = pltpu.CompilerParams(vmem_limit_bytes=40 * 1024 * 1024)

SHARED, OUTER = (0, 1), (2, 3)
CROSS = ((0, 2), (0, 3), (1, 2), (1, 3))
TAIL = 16
RAW_ROWS = 8 * B + TAIL
CODED = 6
HIGH_ROWS = CODED * B
LOW_ROWS = CODED * B // 4
CODE_ROWS = HIGH_ROWS + LOW_ROWS + TAIL
CODE_BITS = 19
LOW_QUADS = (((0, 0, B), (1, 0, B), (2, 0, B), (3, 0, B)), ((4, 0, B // 2), (4, B // 2, B), (5, 0, B // 2), (5, B // 2, B)))
SECOND_ROW, SECOND_COL, ORDER_ONE, ORDER_TWO, FACTS = 0, 1, 2, 6, 10


def pieces(x, count):
    out = []
    for _ in range(count - 1):
        top = x.astype(BF)
        out.append(top)
        x = x - top.astype(F32)
    out.append(x.astype(BF))
    return out


def mm(left, right, order):
    total = None
    for level in range(order, -1, -1):
        for i in range(len(left)):
            j = level - i
            if 0 <= j < len(right):
                term = jnp.dot(left[i], right[j], preferred_element_type=F32)
                total = term if total is None else total + term
    return total


def identity(n):
    return (
        lax.broadcasted_iota(jnp.int32, (n, n), 0) == lax.broadcasted_iota(jnp.int32, (n, n), 1)
    ).astype(F32)


def row_norm(x):
    return jnp.max(jnp.sum(jnp.abs(x), axis=0, keepdims=True), axis=1, keepdims=True)


def solve(level, a, c, c_pieces, r_ref, x_ref, j_ref):
    ratio, steps, goal = level
    n = a.shape[0]
    eye = identity(n)
    picked = a * eye
    down = lax.rsqrt(jnp.sum(picked, axis=1, keepdims=True))
    across = lax.rsqrt(jnp.sum(picked, axis=0, keepdims=True))
    scaled = a * down * across
    j_ref[...] = scaled
    alpha = 2.0 / (row_norm(scaled) * (1.0 + 1.0 / ratio))
    r_ref[...] = eye - alpha * scaled
    x_ref[...] = alpha * eye

    def step(_, t):
        r, x = r_ref[...], x_ref[...]
        rp, xp = pieces(r, 2), pieces(x, 2)
        stacked = [jnp.concatenate([rp[k], xp[k]], axis=0) for k in range(2)]
        prod = mm(stacked, rp, 1)
        t_next = 2.0 * t * t - 1.0
        extra = 1.0 / t_next
        r_ref[...] = prod[:n] * (1.0 + extra) - extra * eye
        x_ref[...] = (x + prod[n:]) * (1.0 + extra)
        return t_next

    first = (ratio + 1.0) / (ratio - 1.0)
    lax.fori_loop(0, steps, step, jnp.full((1, 1), first, F32))

    def unfinished(state):
        count, norm = state
        return (norm > goal) & (count < MOST_STEPS)

    def newton(state):
        count, _ = state
        x = x_ref[...]
        xp = pieces(x, 3)
        r = eye - mm(pieces(j_ref[...], 3), xp, 2)
        x_ref[...] = x + mm(xp, pieces(r, 3), 2)
        norm = jnp.max(row_norm(r))
        return count + 1, jnp.where(norm < 1.0, norm * norm, norm)

    lax.while_loop(unfinished, newton, (jnp.int32(0), jnp.max(row_norm(r_ref[...]))))

    inverse = pieces(x_ref[...] * down * across, 2)
    y = mm(inverse, c_pieces, 1)
    rest = c - mm(pieces(a, 3), pieces(y, 3), 2)
    return y + mm(inverse[:1], pieces(rest, 1), 0)


def others(h0, h1):
    def has(k):
        return (h0 == k) | (h1 == k)

    low = jnp.where(has(0), jnp.where(has(1), 2, 1), 0)
    return low, 6 - h0 - h1 - low


def facts(row, which):
    lanes = lax.broadcasted_iota(jnp.int32, row.shape, 1)
    return [jnp.sum(jnp.where(lanes == k, row, 0.0)).astype(jnp.int32) for k in which]


def at_block(k):
    return pl.ds(pl.multiple_of(k * B, B), B)


def triangles():
    rows = lax.broadcasted_iota(jnp.int32, (B, B), 0)
    cols = lax.broadcasted_iota(jnp.int32, (B, B), 1)
    return rows, cols


def paired(first, second):
    rows, cols = triangles()
    return jnp.where(rows >= cols, first, second)


def diagonal(block):
    rows, cols = triangles()
    return jnp.sum(jnp.where(rows == cols, block, 0.0), axis=0, keepdims=True)


def unpaired(pair, diag):
    rows, cols = triangles()
    turned = pair.T
    first = jnp.where(rows >= cols, pair, turned)
    second = jnp.where(rows == cols, diag, jnp.where(rows < cols, pair, turned))
    return first, second


def symmetric(pair, off, diag):
    d0, d1 = unpaired(pair, diag)
    return square((d0, off, off.T, d1))


def square(blocks):
    w, x, y, z = blocks
    return jnp.concatenate(
        [jnp.concatenate([w, x], axis=1), jnp.concatenate([y, z], axis=1)], axis=0
    )


def block(ref, k):
    return ref[k * B : (k + 1) * B, :].astype(F32)


def tail(ref, start, k):
    return ref[start : start + TAIL, :].astype(F32)[k : k + 1, :]


def raw_shared(ref):
    return symmetric(block(ref, 0), block(ref, 1), tail(ref, 8 * B, 0))


def raw_cross(ref):
    return square([block(ref, 2 + k) for k in range(4)])


def raw_outer(ref):
    return symmetric(block(ref, 6), block(ref, 7), tail(ref, 8 * B, 1))


def ordered(second, own, mate):
    return jnp.concatenate([jnp.where(second, mate, own), jnp.where(second, own, mate)], axis=1)


def outer_diag(second, own_ref, mate_ref):
    own, mate = raw_outer(own_ref), raw_outer(mate_ref)
    zero = jnp.zeros((2 * B, 2 * B), F32)
    top = jnp.concatenate([jnp.where(second, mate, own), zero], axis=1)
    bottom = jnp.concatenate([zero, jnp.where(second, own, mate)], axis=1)
    return jnp.concatenate([top, bottom], axis=0)


def tail_rows(rows):
    at = lax.broadcasted_iota(jnp.int32, (TAIL, B), 0)
    out = jnp.zeros((TAIL, B), rows[0].dtype)
    for k, row in enumerate(rows):
        out = jnp.where(at == k, row, out)
    return out


def whole(x, scale):
    limit = 2.0**CODE_BITS - 1.0
    return jnp.clip(jnp.floor(x * scale + 0.5), -limit, limit).astype(jnp.int32)


def store_code(numbers, row, exponents, ref):
    for k, number in enumerate(numbers):
        ref[k * B : (k + 1) * B, :] = (number >> 4).astype(jnp.int16)
    at = HIGH_ROWS
    for quad in LOW_QUADS:
        w, x, y, z = [numbers[k][start:stop] & 15 for k, start, stop in quad]
        packed = ((w * 16 + x) * 16 + y) * 16 + z - 32768
        ref[at : at + packed.shape[0], :] = packed.astype(jnp.int16)
        at += packed.shape[0]
    rows = [row >> 4, row & 15] + [e.astype(jnp.int32) for e in exponents]
    ref[CODE_ROWS - TAIL : CODE_ROWS, :] = tail_rows(rows).astype(jnp.int16)


def load_code(ref):
    end = ref[CODE_ROWS - TAIL : CODE_ROWS, :].astype(jnp.int32)
    first = ref[HIGH_ROWS : HIGH_ROWS + B, :].astype(jnp.int32) + 32768
    rest = ref[HIGH_ROWS + B : HIGH_ROWS + LOW_ROWS, :].astype(jnp.int32) + 32768
    lows = [(first >> shift) & 15 for shift in (12, 8, 4, 0)]
    halves = [(rest >> shift) & 15 for shift in (12, 8, 4, 0)]
    lows += [jnp.concatenate(halves[k : k + 2], axis=0) for k in (0, 2)]
    numbers = [
        (ref[k * B : (k + 1) * B, :].astype(jnp.int32) * 16 + lows[k]).astype(F32)
        for k in range(CODED)
    ]
    row = (end[0:1, :] * 16 + end[1:2, :]).astype(F32)
    return numbers, row, [end[2 + k : 3 + k, :].astype(F32) for k in range(4)]


def upright(row):
    rows, cols = triangles()
    return jnp.sum(jnp.where(rows == cols, row, 0.0), axis=1, keepdims=True)


def stiff_units(exponents, sign, size):
    across = [jnp.exp2(sign * e) for e in exponents]
    down = [upright(across[k]) * size for k in range(2)]
    units = [paired(down[0] * across[0], down[1] * across[1]), down[0] * across[1]]
    units += [down[i] * across[j] for i, j in CROSS]
    return units, across[1] * across[1] * size


def encode_stiff(blocks, diags, ref):
    exponents = [jnp.ceil(0.5 * jnp.log2(jnp.clip(d, 1e-30, 1e30)) + 2e-3) for d in diags]
    units, unit = stiff_units(exponents, -1.0, 2.0**CODE_BITS)
    numbers = [whole(x, scale) for x, scale in zip(blocks, units)]
    store_code(numbers, whole(diags[1], unit), exponents, ref)


def decode_stiff(ref):
    numbers, row, exponents = load_code(ref)
    units, unit = stiff_units(exponents, 1.0, 2.0**-CODE_BITS)
    blocks = [x * scale for x, scale in zip(numbers, units)]
    return symmetric(blocks[0], blocks[1], row * unit), square(blocks[2:])


def encode_mass(blocks, diag, ref):
    largest = jnp.max(jnp.abs(diag), axis=1, keepdims=True)
    for x in blocks:
        top = jnp.max(jnp.max(jnp.abs(x), axis=0, keepdims=True), axis=1, keepdims=True)
        largest = jnp.maximum(largest, top)
    power = jnp.ceil(jnp.log2(jnp.clip(largest, 1e-30, 1e30)) + 2e-3)
    scale = jnp.exp2(CODE_BITS - power)
    exponent = jnp.zeros((1, B), F32) + power
    store_code([whole(x, scale) for x in blocks], whole(diag, scale), [exponent], ref)


def decode_mass(ref):
    numbers, row, exponents = load_code(ref)
    unit = jnp.exp2(exponents[0][:, 0:1] - CODE_BITS)
    blocks = [x * unit for x in numbers]
    return symmetric(blocks[0], blocks[1], row * unit), square(blocks[2:])


def hand_out(full_ref, a, order, shared_ref, cross_ref, rows_ref):
    d0, off, d1 = [
        full_ref[at_block(order[i]), at_block(order[j])] for i, j in ((0, 0), (0, 1), (1, 1))
    ]
    cross = [full_ref[at_block(order[i]), at_block(order[j])] for i, j in CROSS]
    shared_ref[...] = square((d0, off, off.T, d1))
    cross_ref[...] = square(cross)
    mine = jnp.where(a == 1, order[3], order[2])
    for k in range(2):
        rows_ref[:, k * B : (k + 1) * B] = full_ref[at_block(mine), at_block(order[2 + k])]
    return [paired(d0, d1), off] + cross, [diagonal(d0), diagonal(d1)]


def pair_at(rows, at):
    here = lax.broadcasted_iota(jnp.int32, rows.shape, 1) == at
    held = jnp.where(here, rows.astype(F32), 0.0)
    return [jnp.sum(held[k : k + 1, :]).astype(jnp.int32) for k in range(2)]


def start(copies):
    for copy in copies:
        copy.start()
    return copies


def finish(copies):
    for copy in copies:
        copy.wait()


def pack_kernel(
    axes, prow_hbm, pcol_hbm, one_hbm, two_hbm, k_hbm, m_hbm,
    out_ref, row_gap_ref, col_gap_ref, prow, pcol, one, two, k_ref, m_ref, sems,
):
    pairs = (
        (prow_hbm, prow), (pcol_hbm, pcol), (one_hbm, one), (two_hbm, two), (k_hbm, k_ref), (m_hbm, m_ref)
    )
    copies = start(
        [pltpu.make_async_copy(a, b, sems.at[k]) for k, (a, b) in enumerate(pairs)]
    )
    row, col = lax.axis_index(axes[0]), lax.axis_index(axes[1])
    finish(copies[:4])
    mate, col_mate = prow[row], pcol[col]
    row_gap_ref[0] = (row ^ mate) - 1
    col_gap_ref[0] = (col ^ col_mate) - 1
    h0, h1 = pair_at(one[0], row)
    g0, g1 = pair_at(two[jnp.minimum(row, mate)], col)
    order = (h0, h1) + others(h0, h1)
    known = [(row > mate).astype(jnp.int32), (col > col_mate).astype(jnp.int32), *order]
    known += [g0, g1, *others(g0, g1)]
    lanes = lax.broadcasted_iota(jnp.int32, (1, B), 1)
    noted = jnp.zeros((1, B), F32)
    for k, fact in enumerate(known):
        noted = jnp.where(lanes == k, fact.astype(F32), noted)
    for which, ref in enumerate((k_ref, m_ref)):
        finish([copies[4 + which]])
        for at, (i, j) in ((1, SHARED), (7, OUTER), *((2 + k, pair) for k, pair in enumerate(CROSS))):
            out_ref[which, at * B : (at + 1) * B, :] = ref[at_block(order[i]), at_block(order[j])]
        s0, s1, o0, o1 = [ref[at_block(k), at_block(k)].astype(F32) for k in order]
        out_ref[which, :B, :] = paired(s0, s1).astype(BF)
        out_ref[which, 6 * B : 7 * B, :] = paired(o0, o1).astype(BF)
        out_ref[which, 8 * B :, :] = tail_rows([diagonal(s1), diagonal(o1), noted]).astype(BF)


def one_kernel(
    own, mate,
    fact_ref, x1_ref, code_ref, k_shared, k_cross, k_rows, m_shared, m_cross, m_rows,
    r_ref, x_ref, j_ref, full_k, full_m,
):
    noted = tail(own.at[0], 8 * B, 2)
    fact_ref[...] = jnp.zeros(fact_ref.shape, F32) + noted
    a, *order = facts(noted, (SECOND_ROW, *range(ORDER_TWO, ORDER_TWO + 4)))
    second = noted[:, SECOND_ROW : SECOND_ROW + 1] == 1.0
    own_k, mate_k, own_m, mate_m = own.at[0], mate.at[0], own.at[1], mate.at[1]
    ks = raw_shared(own_k) + raw_shared(mate_k)
    c = ordered(second, raw_cross(own_k), raw_cross(mate_k))
    x = solve(LEVEL_ONE, ks, c, [c.astype(BF)], r_ref, x_ref, j_ref)
    x1_ref[...] = x
    full_k[...] = outer_diag(second, own_k, mate_k) - mm([c.T.astype(BF)], pieces(x, 2), 1)
    xp = pieces(x, 2)
    ms = raw_shared(own_m) + raw_shared(mate_m)
    d = ordered(second, raw_cross(own_m), raw_cross(mate_m))
    w = mm(pieces(ms, 2), xp, 1) - d
    full_m[...] = (
        outer_diag(second, own_m, mate_m)
        + mm(pieces(x.T, 2), pieces(w, 2), 1)
        - mm([d.T.astype(BF)], xp, 1)
    )
    stiff_blocks, stiff_diags = hand_out(full_k, a, order, k_shared, k_cross, k_rows)
    stiff_diags += [diagonal(full_k[at_block(order[k]), at_block(order[k])]) for k in (2, 3)]
    blocks, diags = hand_out(full_m, a, order, m_shared, m_cross, m_rows)
    pl.when(a == 0)(lambda: encode_stiff(stiff_blocks, stiff_diags, code_ref))
    pl.when(a == 1)(lambda: encode_mass(blocks, diags[1], code_ref))


def set_in(second, part):
    zero = jnp.zeros_like(part)
    return jnp.concatenate([jnp.where(second, zero, part), jnp.where(second, part, zero)], axis=1)


def two_kernel(
    fact_ref, got, handed, x1_ref, k_shared, k_cross, k_rows, m_shared, m_cross, m_rows,
    stiff_ref, mass_ref, basis_ref, r_ref, x_ref, j_ref, spread_ref, x2_ref, mate,
):
    noted = fact_ref[:1, :]
    a, b, *order = facts(noted, range(FACTS))
    order_one, order_two = order[:4], order[4:]
    second = noted[:, SECOND_COL : SECOND_COL + 1] == 1.0
    mate[a] = got[...]
    mate[1 - a] = handed[...]
    mate_shared, mate_cross = decode_stiff(mate.at[0])
    ks = k_shared[...] + mate_shared
    c = ordered(second, k_cross[...], mate_cross)
    x = solve(LEVEL_TWO, ks, c, pieces(c, 2), r_ref, x_ref, j_ref)
    x2_ref[...] = x
    xp = pieces(x, 2)
    c_mine = k_cross[:, at_block(a)]
    stiff_ref[...] = set_in(second, k_rows[...]) - mm(pieces(c_mine.T, 2), xp, 1)

    mate_shared, mate_cross = decode_mass(mate.at[1])
    ms = m_shared[...] + mate_shared
    d = ordered(second, m_cross[...], mate_cross)
    w = mm(pieces(ms, 2), xp, 1) - d
    x_mine = x2_ref[:, at_block(2 * b + a)]
    d_mine = m_cross[:, at_block(a)]
    mass_ref[...] = (
        set_in(second, m_rows[...])
        + mm(pieces(x_mine.T, 2), pieces(w, 2), 1)
        - mm(pieces(d_mine.T, 2), xp, 1)
    )

    eye = identity(B)
    zero = jnp.zeros((B, B), F32)
    for k in range(2):
        spread_ref[at_block(order_two[k]), :] = -x[k * B : (k + 1) * B, :]
        half = jnp.concatenate([eye if k == 0 else zero, eye if k == 1 else zero], axis=1)
        spread_ref[at_block(order_two[2 + k]), :] = set_in(second, half)
    for k in range(2):
        basis_ref[at_block(order_one[2 + k]), :] = spread_ref[at_block(2 * a + k), :]
    x1_sh = jnp.concatenate([x1_ref[:, at_block(order_two[k])] for k in range(2)], axis=1)
    x1_out = jnp.concatenate([x1_ref[:, at_block(order_two[2 + k])] for k in range(2)], axis=1)
    shared = mm(pieces(x1_sh, 2), xp, 1) - set_in(second, x1_out)
    for k in range(2):
        basis_ref[at_block(order_one[k]), :] = shared[k * B : (k + 1) * B, :]


def call(kernel, outs, scratch, arrays):
    return pl.pallas_call(
        kernel,
        out_shape=[jax.ShapeDtypeStruct(shape, dtype) for shape, dtype in outs],
        in_specs=[VMEM] * len(arrays),
        out_specs=[VMEM] * len(outs),
        scratch_shapes=[pltpu.VMEM(shape, dtype) for shape, dtype in scratch],
        compiler_params=PARAMS,
        cost_estimate=pl.CostEstimate(flops=6 << 30, bytes_accessed=1 << 22, transcendentals=0),
    )(*arrays)


def swap(axis, size, gap, array):
    def branch(apart):
        return lambda y: lax.ppermute(y, axis, [(i, i ^ apart) for i in range(size)])

    return lax.switch(gap, [branch(apart) for apart in range(1, size)], array)


def local(stiff, mass, partner_row, partner_col, shared_one, shared_two):
    iface = stiff.shape[0]
    half = iface // 2
    square_half = ((half, half), F32)
    n_row, n_col = partner_row.shape[0], partner_col.shape[0]
    raw = ((2, RAW_ROWS, B), BF)
    code = ((CODE_ROWS, B), jnp.int16)
    codes = ((2, CODE_ROWS, B), jnp.int16)

    packed, row_gap, col_gap = pl.pallas_call(
        functools.partial(pack_kernel, ("row", "col")),
        out_shape=[
            jax.ShapeDtypeStruct(*raw),
            jax.ShapeDtypeStruct((1,), jnp.int32),
            jax.ShapeDtypeStruct((1,), jnp.int32),
        ],
        in_specs=[HBM] * 6,
        out_specs=[VMEM, SMEM, SMEM],
        scratch_shapes=[
            pltpu.SMEM((n_row,), jnp.int32),
            pltpu.SMEM((n_col,), jnp.int32),
            pltpu.VMEM((1, 2, n_row), jnp.int32),
            pltpu.VMEM((n_row, 2, n_col), jnp.int32),
            pltpu.VMEM(stiff.shape, BF),
            pltpu.VMEM(mass.shape, BF),
            pltpu.SemaphoreType.DMA((6,)),
        ],
        compiler_params=pltpu.CompilerParams(vmem_limit_bytes=60 * 1024 * 1024),
    )(
        partner_row, partner_col,
        jnp.transpose(shared_one, (1, 2, 0)), jnp.transpose(shared_two, (0, 2, 1)), stiff, mass,
    )
    mate = swap("row", n_row, row_gap.reshape(()), packed)
    row_gap, col_gap = row_gap.reshape(()), col_gap.reshape(())
    known, x1, sent, *kept = call(
        one_kernel,
        [((8, B), F32), ((half, iface), F32), code] + [square_half, square_half, ((B, half), F32)] * 2,
        [square_half] * 3 + [((iface, iface), F32)] * 2,
        (packed, mate),
    )
    got = swap("col", n_col, col_gap, sent)
    handed = swap("row", n_row, row_gap, got)
    return tuple(
        call(
            two_kernel,
            [((B, iface), F32), ((B, iface), F32), ((iface, iface), F32)],
            [square_half] * 3 + [((iface, iface), F32), ((half, iface), F32), codes],
            (known, got, handed, x1, *kept),
        )
    )


def solution(mesh):
    return jax.shard_map(
        local,
        mesh=mesh,
        in_specs=(P("row", "col"), P("row", "col"), P(), P(), P(None, "col", None), P()),
        out_specs=(P("row", "col"), P("row", "col"), P("row", "col")),
        check_vma=False,
    )
```
